128 devices in a mesh: row: 16 (over x, z_hi, core), col: 8 (over z_lo, y).
Axes of the slice: x: 4, y: 4, z: 4 (z_hi: 2, z_lo: 2; z = z_hi * 2 + z_lo), core: 2. Of those that a mesh axis runs over, the one named last changes fastest.
Arguments:
- homolog_embedding: bfloat16 [128, 1024, 256], P(None, ('row', 'col')), may hold values from -6 to 6
- standardizer_multiplier: float32 [256], replicated, may hold values from 0.5 to 1.5
- first_factor_matrix: bfloat16 [256, 32], replicated, may hold values from -0.375 to 0.375
- second_factor_matrix: bfloat16 [256, 32], replicated, may hold values from -0.375 to 0.375
- output_weight: bfloat16 [1024, 128], replicated, may hold values from -2.09375 to 2.09375
- cotangent: bfloat16 [1024, 16, 64, 128], P('row', None, 'col'), may hold values from -6 to 6
Outputs:
- pair_update_tiles: bfloat16 [1024, 16, 64, 128], P('row', None, 'col')
- alignment_gradient: bfloat16 [128, 1024, 256], P(None, ('row', 'col'))
- left_weight_gradient: float32 [256, 32], replicated
- right_weight_gradient: float32 [256, 32], replicated
- output_weight_gradient: float32 [1024, 128], replicated
- norm_gain_gradient: float32 [256], replicated
The draws below stay inside these ranges and needn't reach their ends.
All inputs are finite; a program needn't handle non-finite values.
Results may differ from the reference program's by a relative error of at most 0.0079.
Values may be sent and summed in bfloat16 or wider, within the bound.
A program may use at most 128 MiB of HBM per device.

```python
import math
import jax
import jax.numpy as jnp
from jax import lax

EMBED_DIMENSION = 256
PROJECTION_WIDTH = 32
CZ = 128
HOMOLOG_NUMBER = 128
CHAIN_LENGTH = 1024
CC = 1024
N_ROW = 16


def steps_of(rng, shape, cuts, smallest, top_value):
    def one(position, shards_of):
        draws = jax.random.uniform(jax.random.fold_in(jax.random.fold_in(rng, 6), position), (shards_of,), jnp.float32, smallest / len(cuts), top_value / len(cuts))
        return jnp.repeat(jnp.exp(draws), shape[position] // shards_of).reshape((-1,) + (1,) * (len(shape) - position - 1))

    loudness = one(*cuts[0])
    for cut in cuts[1:]:
        loudness = loudness * one(*cut)
    return loudness


def centred(rng, extent, spread, most, pieces=(), dtype=jnp.bfloat16):
    values = jax.random.normal(rng, extent, jnp.float32) * spread
    if len(pieces) > 0:
        values = steps_of(rng, extent, pieces, -0.22, 0.18) * values
    return jnp.clip(values, min=-most, max=most).astype(dtype)


def setup_inputs(seed: int = 0) -> dict:
    seeds = jax.random.split(jax.random.key(seed), 7)
    return {
        "homolog_embedding": centred(seeds[0], (HOMOLOG_NUMBER, CHAIN_LENGTH, EMBED_DIMENSION), 1.0, 6.0, ((1, 128),)),
        "standardizer_multiplier": jnp.clip(1.0 + 0.1 * jax.random.normal(seeds[1], (EMBED_DIMENSION,), jnp.float32), 0.5, 1.5),
        "first_factor_matrix": centred(seeds[2], (EMBED_DIMENSION, PROJECTION_WIDTH), EMBED_DIMENSION ** -0.5, 0.375),
        "second_factor_matrix": centred(seeds[3], (EMBED_DIMENSION, PROJECTION_WIDTH), EMBED_DIMENSION ** -0.5, 0.375),
        "output_weight": centred(seeds[4], (CC, CZ), 0.35, 2.09375),
        "cotangent": centred(seeds[5], (CHAIN_LENGTH, N_ROW, CHAIN_LENGTH // N_ROW, CZ), 1.0, 6.0, ((0, 16), (2, 8))),
    }


def apply_layer_norm(values, standardizer_multiplier):
    inputs = values.astype(jnp.float32)
    center = inputs - lax.optimization_barrier(jnp.mean(inputs, axis=-1, keepdims=True))
    inverse_deviation = lax.rsqrt(lax.optimization_barrier(jnp.mean(center * center, axis=-1, keepdims=True)) + 1e-05)
    scaled = center * inverse_deviation
    return (scaled, inverse_deviation, (scaled * standardizer_multiplier).astype(jnp.bfloat16))

def project(standardized_embedding, weight):
    flat = standardized_embedding.reshape(-1, standardized_embedding.shape[2])
    result = jnp.dot(flat, weight, preferred_element_type=jnp.float32).astype(jnp.bfloat16)
    return jnp.transpose(result.reshape(standardized_embedding.shape[0], standardized_embedding.shape[1], -1), (1, 2, 0))

def reference(homolog_embedding, standardizer_multiplier, first_factor_matrix, second_factor_matrix, output_weight, cotangent):
    centered_scaled, inverse_deviation, standardized_embedding = apply_layer_norm(homolog_embedding, standardizer_multiplier)
    left_all = project(standardized_embedding, first_factor_matrix)
    right_all = project(standardized_embedding, second_factor_matrix)
    block_rows = math.gcd(CHAIN_LENGTH, 64)
    nblocks = CHAIN_LENGTH // block_rows
    left_blocks = left_all.reshape(nblocks, block_rows, PROJECTION_WIDTH, HOMOLOG_NUMBER)
    cot_blocks = cotangent.reshape(nblocks, block_rows, CHAIN_LENGTH, CZ)
    right_wide = right_all.astype(jnp.float32)

    def one_block(carry, inputs):
        grad_wout, grad_right = carry
        left_block, cot_block = inputs
        outer_b = jnp.einsum('ics,jes->ijce', left_block.astype(jnp.float32), right_wide).astype(jnp.bfloat16)
        outer_flat = outer_b.reshape(-1, CC)
        pair_blk = (jnp.dot(outer_flat, output_weight, preferred_element_type=jnp.float32) / HOMOLOG_NUMBER).astype(jnp.bfloat16)
        cot_flat = cot_block.reshape(-1, CZ)
        grad_outer = (jnp.dot(cot_flat, output_weight.T, preferred_element_type=jnp.float32) / HOMOLOG_NUMBER).astype(jnp.bfloat16)
        grad_outer = grad_outer.reshape(block_rows, CHAIN_LENGTH, PROJECTION_WIDTH, PROJECTION_WIDTH).astype(jnp.float32)
        grad_wout = grad_wout + jnp.dot(outer_flat.T, cot_flat, preferred_element_type=jnp.float32)
        left_part = jnp.einsum('ijce,jes->ics', grad_outer, right_wide)
        grad_right = grad_right + jnp.einsum('ijce,ics->jes', grad_outer, left_block.astype(jnp.float32))
        return ((grad_wout, grad_right), (pair_blk.reshape(block_rows, CHAIN_LENGTH, CZ), left_part))
    start = (jnp.zeros((CC, CZ), jnp.float32), jnp.zeros((CHAIN_LENGTH, PROJECTION_WIDTH, HOMOLOG_NUMBER), jnp.float32))
    (grad_wout, grad_right), (pairs, left_parts) = lax.scan(one_block, start, (left_blocks, cot_blocks))
    pair_update_tiles = pairs.reshape(CHAIN_LENGTH, N_ROW, CHAIN_LENGTH // N_ROW, CZ)
    output_weight_gradient = grad_wout / HOMOLOG_NUMBER
    d_left = jnp.transpose(left_parts.reshape(CHAIN_LENGTH, PROJECTION_WIDTH, HOMOLOG_NUMBER).astype(jnp.bfloat16), (2, 0, 1))
    d_right = jnp.transpose(grad_right.astype(jnp.bfloat16), (2, 0, 1))
    standardized_matrix_view = standardized_embedding.reshape(-1, EMBED_DIMENSION)
    dleft_flat = d_left.reshape(-1, PROJECTION_WIDTH)
    dright_flat = d_right.reshape(-1, PROJECTION_WIDTH)
    left_weight_gradient = jnp.dot(standardized_matrix_view.T, dleft_flat, preferred_element_type=jnp.float32)
    right_weight_gradient = jnp.dot(standardized_matrix_view.T, dright_flat, preferred_element_type=jnp.float32)
    standardized_cotangent = jnp.dot(dleft_flat, first_factor_matrix.T, preferred_element_type=jnp.float32) + jnp.dot(dright_flat, second_factor_matrix.T, preferred_element_type=jnp.float32)
    standardized_cotangent = standardized_cotangent.reshape(HOMOLOG_NUMBER, CHAIN_LENGTH, EMBED_DIMENSION)
    norm_gain_gradient = lax.optimization_barrier(jnp.sum(standardized_cotangent * centered_scaled, axis=(0, 1)))
    hidden_features = standardized_cotangent * standardizer_multiplier
    alignment_gradient = inverse_deviation * (hidden_features - lax.optimization_barrier(jnp.mean(hidden_features, axis=-1, keepdims=True)) - centered_scaled * lax.optimization_barrier(jnp.mean(hidden_features * centered_scaled, axis=-1, keepdims=True)))
    return (pair_update_tiles, alignment_gradient.astype(jnp.bfloat16), left_weight_gradient, right_weight_gradient, output_weight_gradient, norm_gain_gradient)
```

```python
import functools

import jax
import jax.numpy as jnp
from jax import lax
from jax.experimental import pallas as pl
from jax.experimental.pallas import tpu as pltpu
from jax.sharding import PartitionSpec as P

MESH = pl.DeviceIdType.MESH
BF = jnp.bfloat16
F32 = jnp.float32
NT = (((1,), (1,)), ((), ()))
TN = (((0,), (0,)), ((), ()))


def mm(a, b):
    return jnp.dot(a, b, preferred_element_type=F32)


def mm_nt(a, b):
    return lax.dot_general(a, b, NT, preferred_element_type=F32)


def mm_tn(a, b):
    return lax.dot_general(a, b, TN, preferred_element_type=F32)


def remote(src, dst, send_sem, recv_sem, **where):
    return pltpu.make_async_remote_copy(
        src_ref=src, dst_ref=dst, send_sem=send_sem, recv_sem=recv_sem,
        device_id=where, device_id_type=MESH,
    )


def aligned(start, size, multiple):
    return pl.ds(pl.multiple_of(start, multiple), size)


def kernel(
    n_row, n_col,
    x_ref, gamma_ref, w1_ref, w2_ref, wo_ref, g_hbm,
    z_hbm, ag_ref, wl_ref, wr_ref, dwo_ref, gain_ref,
    g_ref, xs, xh, nm, rs, wp, wpt, wf, rf, right_in, right, left, left_t, buf,
    dl_out, dl_in, dr_out, dr_sib, dr_in, dl_own, dr_own,
    dw_acc, dw_out, dw_in, dw_blk, dw_col, dw_full,
    sm_out, sm_in, sm_blk, sm_col, sm_full, z_buf,
    g_sem, z_sem,
    rg_s, rg_r, lg_s, lg_r, dl_s, dl_r, sib_s, sib_r, dr_s, dr_r,
    w1_s, w1_r, w2_s, w2_r, w3_s, w3_r, s1_s, s1_r, s2_s, s2_r, s3_s, s3_r,
):
    S, T, M = x_ref.shape
    C = w1_ref.shape[0]
    CC, K = wo_ref.shape
    J = n_row * T
    I = n_col * T
    B = T * C
    n_chip = n_row // 2
    inv = 1.0 / S
    row = lax.axis_index("row")
    col = lax.axis_index("col")
    chip = row // 2
    core = lax.rem(row, 2)
    sib = chip * 2 + 1 - core
    pending = []

    def send(c):
        c.start()
        pending.append(c)

    def other_row(d):
        return lax.rem(row + d, n_row)

    def other_col(d):
        return lax.rem(col + d, n_col)

    def other_chip(d):
        return lax.rem(chip + d, n_chip)

    barrier = pltpu.get_barrier_semaphore()
    for d in range(1, n_row):
        pl.semaphore_signal(barrier, inc=1, device_id={"row": other_row(d)}, device_id_type=MESH)
    for d in range(1, n_col):
        pl.semaphore_signal(barrier, inc=1, device_id={"col": other_col(d)}, device_id_type=MESH)

    g_copy = pltpu.make_async_copy(g_hbm, g_ref, g_sem)
    g_copy.start()

    wcat = jnp.concatenate([w1_ref[...], w2_ref[...]], axis=0)
    gamma = gamma_ref[...]
    wide = M // K
    x_all = x_ref[...].astype(F32).reshape(S * T, M)
    for a in range(wide):
        xs[a] = x_all[:, a * K:(a + 1) * K]
    for t in range(T):
        xt = jnp.concatenate([xs[a, pl.ds(t, S, stride=T), :] for a in range(wide)], axis=1)
        center = xt - jnp.mean(xt, axis=1, keepdims=True)
        rstd = lax.rsqrt(jnp.mean(center * center, axis=1, keepdims=True) + 1e-05)
        xhat = center * rstd
        normed = (xhat * gamma).astype(BF)
        xh[t] = xhat
        nm[t] = normed
        rs[t] = jnp.broadcast_to(rstd, (S, K))
        proj = mm_nt(wcat, normed)
        left[aligned(col * B + t * C, C, C), :] = proj[:C].astype(BF)
        rf[pl.ds(t, C, stride=T), :] = proj[C:]
    right_in[row] = rf[...].astype(BF)

    pl.semaphore_wait(barrier, n_row + n_col - 2)

    send(remote(right_in.at[row], right_in.at[row], rg_s.at[0], rg_r.at[row], row=sib))
    for d in range(1, n_chip):
        peer = other_chip(d) * 2 + core
        send(remote(right_in.at[row], right_in.at[row], rg_s.at[d], rg_r.at[row], row=peer))
    mine = aligned(col * B, B, B)
    for d in range(1, n_col):
        send(remote(left.at[mine], left.at[mine], lg_s.at[d], lg_r.at[col], col=other_col(d)))

    wf[...] = wo_ref[...].astype(F32)
    for e in range(C):
        wp[e * C:(e + 1) * C, :] = wf[pl.ds(e, C, stride=C), :].astype(BF)
    wpt[...] = wp[...].astype(F32).T.astype(BF)

    g_copy.wait()
    def go_step(p, _):
        res = mm_nt(wp[...], g_ref[aligned(p * 2 * J, 2 * J, 2 * J), :]).astype(BF)
        for a in range(2):
            for e in range(C):
                buf[aligned((2 * p + a) * C, C, C), e * J:(e + 1) * J] = (
                    res[e * C:(e + 1) * C, a * J:(a + 1) * J]
                )
        return 0
    lax.fori_loop(0, I // 2, go_step, 0)

    for d in range(1, n_chip):
        src = lax.rem(chip + n_chip - d, n_chip) * 2 + core
        remote(right_in.at[src], right_in.at[src], rg_s.at[d], rg_r.at[src], row=src).wait_recv()
        send(remote(right_in.at[src], right_in.at[src], rg_s.at[n_chip + d], rg_r.at[src], row=sib))
    remote(right_in.at[sib], right_in.at[sib], rg_s.at[0], rg_r.at[sib], row=sib).wait_recv()
    for d in range(1, n_chip):
        src = lax.rem(chip + n_chip - d, n_chip) * 2 + 1 - core
        remote(right_in.at[src], right_in.at[src], rg_s.at[0], rg_r.at[src], row=sib).wait_recv()

    def right_step(h, _):
        parts = [right_in[q, aligned(h * 2 * T, 2 * T, 2 * T), :].astype(F32) for q in range(n_row)]
        for a in range(2):
            tile = jnp.concatenate([p[a * T:(a + 1) * T] for p in parts], axis=0)
            right[aligned((2 * h + a) * J, J, J), :] = tile.astype(BF)
        return 0
    lax.fori_loop(0, C // 2, right_step, 0)

    def dl_step(k, _):
        owner = lax.rem(col + 1 + k, n_col)
        part = mm(buf[aligned(owner * B, B, B), :], right[...]) * inv
        dl_out[owner] = part.astype(BF)
        return 0
    for k in range(n_col):
        dl_step(k, 0)
        if k < n_col - 1:
            owner = other_col(k + 1)
            send(remote(dl_out.at[owner], dl_in.at[col], dl_s.at[k], dl_r.at[col], col=owner))

    for d in range(1, n_col):
        src = lax.rem(col + n_col - d, n_col)
        rows = aligned(src * B, B, B)
        remote(left.at[rows], left.at[rows], lg_s.at[d], lg_r.at[src], col=src).wait_recv()
    def turn_step(k, _):
        rows = aligned(k * B, B, B)
        left_t[k] = left[rows, :].astype(F32).T.astype(BF)
        return 0
    lax.fori_loop(0, n_col, turn_step, 0)

    def dr_step(h, _):
        lanes = aligned(h * 2 * J, 2 * J, 2 * J)
        acc = mm(left_t[0], buf[0:B, lanes])
        for k in range(1, n_col):
            acc = acc + mm(left_t[k], buf[k * B:(k + 1) * B, lanes])
        acc = acc * inv
        tiles = [acc[:, a * J:(a + 1) * J].T for a in range(2)]
        for q in range(n_row):
            blk = jnp.concatenate([t[q * T:(q + 1) * T] for t in tiles], axis=0)
            dr_out[q % 2, q // 2, aligned(h * 2 * T, 2 * T, 2 * T), :] = blk.astype(BF)
        return 0
    lax.fori_loop(0, C // 2, dr_step, 0)
    to_sib = remote(dr_out.at[1 - core], dr_sib, sib_s, sib_r, row=sib)
    send(to_sib)

    RB = 2 * B
    NB = 4 * J
    def outer_step(k, _):
        rows = aligned(k * RB, RB, RB)
        for n in range(C * J // NB):
            res = mm_nt(left[rows, :], right[n * NB:(n + 1) * NB, :])
            buf[rows, n * NB:(n + 1) * NB] = res.astype(BF)
        return 0
    lax.fori_loop(0, I * C // RB, outer_step, 0)

    to_sib.wait_recv()
    def pair_step(q, _):
        dr_sib[q] = (dr_out[core, q].astype(F32) + dr_sib[q].astype(F32)).astype(BF)
        return 0
    lax.fori_loop(0, n_chip, pair_step, 0)
    for d in range(1, n_chip):
        peer = other_chip(d)
        send(remote(dr_sib.at[peer], dr_in.at[chip], dr_s.at[d], dr_r.at[chip], row=peer * 2 + core))

    EH = C // 2
    RW = CC // n_row
    for h in range(2):
        dw_acc[...] = jnp.zeros_like(dw_acc)
        def dw_step(p, _):
            acc = None
            for b in range(2):
                lhs = jnp.concatenate([
                    jnp.concatenate([
                        buf[aligned((4 * p + 2 * b + a) * C, C, C), e * J:(e + 1) * J]
                        for e in range(h * EH, (h + 1) * EH)], axis=0)
                    for a in range(2)], axis=1)
                res = mm(lhs, g_ref[aligned((4 * p + 2 * b) * J, 2 * J, 2 * J), :])
                acc = res if acc is None else acc + res
            dw_acc[...] += acc
            return 0
        lax.fori_loop(0, I // 4, dw_step, 0)
        half = n_row // 2
        dw_out[h * half:(h + 1) * half] = dw_acc[...].astype(BF).reshape(half, RW, K)
    for d in range(1, n_row):
        peer = other_row(d)
        send(remote(dw_out.at[peer], dw_in.at[row], w1_s.at[d], w1_r.at[row], row=peer))

    dl_sum = dl_out[col].astype(F32)
    for d in range(1, n_col):
        src = lax.rem(col + n_col - d, n_col)
        remote(dl_in.at[src], dl_in.at[src], dl_s.at[0], dl_r.at[src], col=src).wait_recv()
        dl_sum = dl_sum + dl_in[src].astype(F32)
    dl_own[...] = dl_sum.astype(BF)
    dr_sum = dr_sib[chip].astype(F32)
    for d in range(1, n_chip):
        src = lax.rem(chip + n_chip - d, n_chip)
        remote(dr_in.at[src], dr_in.at[src], dr_s.at[d], dr_r.at[src], row=src * 2 + core).wait_recv()
        dr_sum = dr_sum + dr_in[src].astype(F32)
    dr_own[...] = dr_sum

    gain = jnp.zeros((1, M), F32)
    wgrad = jnp.zeros((2 * C, M), F32)
    for t in range(T):
        dcat = jnp.concatenate(
            [dl_own[t * C:(t + 1) * C, :], dr_own[pl.ds(t, C, stride=T), :].astype(BF)], axis=0)
        wgrad = wgrad + mm(dcat, nm[t])
        dn = mm_tn(dcat, wcat)
        xhat = xh[t]
        gain = gain + jnp.sum(dn * xhat, axis=0, keepdims=True)
        hid = dn * gamma
        m1 = jnp.mean(hid, axis=1, keepdims=True)
        m2 = jnp.mean(hid * xhat, axis=1, keepdims=True)
        rstd = rs[t]
        rstd = jnp.concatenate([rstd] * wide, axis=1)
        grad = rstd * (hid - m1 - xhat * m2)
        for a in range(wide):
            xs[a, pl.ds(t, S, stride=T), :] = grad[:, a * K:(a + 1) * K]
    grads = jnp.concatenate([xs[a] for a in range(wide)], axis=1)
    ag_ref[...] = grads.reshape(S, T, M).astype(BF)

    RS = 2 * C * wide // n_row
    gain_rows = jnp.concatenate([gain[:, a * K:(a + 1) * K] for a in range(wide)]
                                + [jnp.zeros((8 - wide, K), F32)], axis=0)
    for q in range(n_row):
        a, r0 = divmod(q * RS, 2 * C)
        sm_out[q, 0:RS, :] = wgrad[r0:r0 + RS, a * K:(a + 1) * K]
        sm_out[q, RS:RS + 8, :] = gain_rows
    for d in range(1, n_row):
        peer = other_row(d)
        send(remote(sm_out.at[peer], sm_in.at[row], s1_s.at[d], s1_r.at[row], row=peer))

    def sum_row(own, got, ss, rr):
        total = own.astype(F32)
        for d in range(1, n_row):
            src = lax.rem(row + n_row - d, n_row)
            remote(got.at[src], got.at[src], ss.at[d], rr.at[src], row=src).wait_recv()
            total = total + got[src].astype(F32)
        return total

    def sum_col(own, got, ss, rr):
        total = own
        for d in range(1, n_col):
            src = lax.rem(col + n_col - d, n_col)
            remote(got.at[src], got.at[src], ss.at[d], rr.at[src], col=src).wait_recv()
            total = total + got[src]
        return total

    def z_step(p, _):
        rhs = jnp.concatenate([
            jnp.concatenate([
                buf[aligned((2 * p + a) * C, C, C), e * J:(e + 1) * J] for e in range(C)], axis=0)
            for a in range(2)], axis=1)
        res = mm(wpt[...], rhs) * inv
        for a in range(2):
            z_buf[aligned((2 * p + a) * J, J, J), :] = res[:, a * J:(a + 1) * J].T.astype(BF)
        return 0

    z_copies = []
    def z_part(n, of):
        lo, hi = n * (I // 2) // of, (n + 1) * (I // 2) // of
        lax.fori_loop(lo, hi, z_step, 0)
        rows = pl.ds(lo * 2 * J, (hi - lo) * 2 * J)
        c = pltpu.make_async_copy(z_buf.at[rows], z_hbm.at[rows], z_sem.at[n])
        c.start()
        z_copies.append(c)

    dw_blk[0] = sum_row(dw_out[row], dw_in, w1_s, w1_r)
    for d in range(1, n_col):
        send(remote(dw_blk.at[0], dw_col.at[col], w2_s.at[d], w2_r.at[col], col=other_col(d)))
    z_part(0, 4)
    sm_blk[...] = sum_row(sm_out[row], sm_in, s1_s, s1_r)
    for d in range(1, n_col):
        send(remote(sm_blk, sm_col.at[col], s2_s.at[d], s2_r.at[col], col=other_col(d)))
    z_part(1, 4)
    dw_blk[1] = sum_col(dw_blk[0], dw_col, w2_s, w2_r) * inv
    dw_full[row] = dw_blk[1]
    for d in range(1, n_row):
        send(remote(dw_blk.at[1], dw_full.at[row], w3_s.at[d], w3_r.at[row], row=other_row(d)))
    z_part(2, 4)
    sm_full[row] = sum_col(sm_blk[...], sm_col, s2_s, s2_r)
    for d in range(1, n_row):
        send(remote(sm_full.at[row], sm_full.at[row], s3_s.at[d], s3_r.at[row], row=other_row(d)))
    z_part(3, 4)

    for d in range(1, n_row):
        src = lax.rem(row + n_row - d, n_row)
        remote(dw_full.at[src], dw_full.at[src], w3_s.at[d], w3_r.at[src], row=src).wait_recv()
    for e in range(C):
        q, r0 = divmod(e * C, RW)
        dwo_ref[pl.ds(e, C, stride=C), :] = dw_full[q, r0:r0 + C, :]
    for d in range(1, n_row):
        src = lax.rem(row + n_row - d, n_row)
        remote(sm_full.at[src], sm_full.at[src], s3_s.at[d], s3_r.at[src], row=src).wait_recv()
    for q in range(n_row):
        a, r0 = divmod(q * RS, 2 * C)
        for out, lo in ((wl_ref, 0), (wr_ref, C)):
            if lo <= r0 < lo + C:
                out[r0 - lo:r0 - lo + RS, a * K:(a + 1) * K] = sm_full[q, 0:RS, :]
    for a in range(wide):
        gain_ref[:, a * K:(a + 1) * K] = sm_full[0, RS + a:RS + a + 1, :]

    for c in z_copies:
        c.wait()
    for c in pending:
        c.wait_send()


def on_device(n_row, n_col, x, gamma, w1, w2, wo, cot):
    S, T, M = x.shape
    C = w1.shape[1]
    CC, K = wo.shape
    I, J = cot.shape[0], cot.shape[1] * cot.shape[2]
    B = T * C
    n_chip = n_row // 2
    RW = CC // n_row
    RS = 2 * C * (M // K) // n_row
    V = lambda shape, dtype: pltpu.VMEM(shape, dtype)
    D = lambda n: pltpu.SemaphoreType.DMA((n,))
    vm = pl.BlockSpec(memory_space=pltpu.VMEM)
    hb = pl.BlockSpec(memory_space=pl.ANY)
    z, ag, wl, wr, dwo, gain = pl.pallas_call(
        functools.partial(kernel, n_row, n_col),
        out_shape=(
            jax.ShapeDtypeStruct((I * J, K), BF),
            jax.ShapeDtypeStruct((S, T, M), BF),
            jax.ShapeDtypeStruct((C, M), F32),
            jax.ShapeDtypeStruct((C, M), F32),
            jax.ShapeDtypeStruct((CC, K), F32),
            jax.ShapeDtypeStruct((1, M), F32),
        ),
        in_specs=[vm, vm, vm, vm, vm, hb],
        out_specs=(hb, vm, vm, vm, vm, vm),
        scratch_shapes=[
            V((I * J, K), BF),
            V((M // K, S * T, K), F32),
            V((T, S, M), F32),
            V((T, S, M), BF),
            V((T, S, K), F32),
            V((CC, K), BF),
            V((K, CC), BF),
            V((CC, K), F32),
            V((B, S), F32),
            V((n_row, B, S), BF),
            V((C * J, S), BF),
            V((I * C, S), BF),
            V((n_col, S, B), BF),
            V((I * C, C * J), BF),
            V((n_col, B, S), BF),
            V((n_col, B, S), BF),
            V((2, n_chip, B, S), BF),
            V((n_chip, B, S), BF),
            V((n_chip, B, S), BF),
            V((B, S), BF),
            V((B, S), F32),
            V((CC // 2, K), F32),
            V((n_row, RW, K), BF),
            V((n_row, RW, K), BF),
            V((2, RW, K), F32),
            V((n_col, RW, K), F32),
            V((n_row, RW, K), F32),
            V((n_row, RS + 8, K), F32),
            V((n_row, RS + 8, K), F32),
            V((RS + 8, K), F32),
            V((n_col, RS + 8, K), F32),
            V((n_row, RS + 8, K), F32),
            V((I * J, K), BF),
            pltpu.SemaphoreType.DMA,
            D(4),
            D(n_row), D(n_row), D(n_col), D(n_col), D(n_col), D(n_col),
            pltpu.SemaphoreType.DMA, pltpu.SemaphoreType.DMA, D(n_chip), D(n_chip),
            D(n_row), D(n_row), D(n_col), D(n_col), D(n_row), D(n_row),
            D(n_row), D(n_row), D(n_col), D(n_col), D(n_row), D(n_row),
        ],
        compiler_params=pltpu.CompilerParams(
            collective_id=0, has_side_effects=True, vmem_limit_bytes=56 * 1024 * 1024,
        ),
    )(x, gamma.reshape(1, M), w1.T, w2.T, wo, cot.reshape(I * J, K))
    return z.reshape(cot.shape), ag, wl.T, wr.T, dwo, gain.reshape(M)


def solution(mesh):
    placed = (P(None, ("row", "col"), None), P(), P(), P(), P(), P("row", None, "col", None))
    return jax.shard_map(
        functools.partial(on_device, mesh.shape["row"], mesh.shape["col"]),
        mesh=mesh,
        in_specs=placed,
        out_specs=(P("row", None, "col", None), P(None, ("row", "col"), None), P(), P(), P(), P()),
        check_vma=False,
    )
```

```python
import functools

import jax
import jax.numpy as jnp
from jax import lax
from jax.experimental import pallas as pl
from jax.experimental.pallas import tpu as pltpu
from jax.sharding import PartitionSpec as P

MESH = pl.DeviceIdType.MESH
BF = jnp.bfloat16
F32 = jnp.float32
NT = (((1,), (1,)), ((), ()))
TN = (((0,), (0,)), ((), ()))


def mm(a, b):
    return jnp.dot(a, b, preferred_element_type=F32)


def mm_nt(a, b):
    return lax.dot_general(a, b, NT, preferred_element_type=F32)


def mm_tn(a, b):
    return lax.dot_general(a, b, TN, preferred_element_type=F32)


def remote(src, dst, send_sem, recv_sem, **where):
    return pltpu.make_async_remote_copy(
        src_ref=src, dst_ref=dst, send_sem=send_sem, recv_sem=recv_sem,
        device_id=where, device_id_type=MESH,
    )


def aligned(start, size, multiple):
    return pl.ds(pl.multiple_of(start, multiple), size)


def kernel(
    n_row, n_col,
    x_ref, gamma_ref, w1_ref, w2_ref, wo_ref, g_hbm,
    z_hbm, ag_ref, wl_ref, wr_ref, dwo_ref, gain_ref,
    g_ref, xs, xh, nm, rs, wp, wpt, wf, rf, right_in, right, left, left_t, g_out, buf,
    dl_out, dl_in, dr_out, dr_sib, dr_in, dl_own, dr_own,
    dw_out, dw_in, dw_blk, dw_col, dw_full,
    sm_out, sm_in, sm_blk, sm_col, sm_full, z_buf,
    g_sem, z_sem,
    rg_s, rg_r, lg_s, lg_r, dl_s, dl_r, sib_s, sib_r, dr_s, dr_r,
    w1_s, w1_r, w2_s, w2_r, w3_s, w3_r, s1_s, s1_r, s2_s, s2_r, s3_s, s3_r,
):
    S, T, M = x_ref.shape
    C = w1_ref.shape[0]
    CC, K = wo_ref.shape
    J = n_row * T
    I = n_col * T
    B = T * C
    n_chip = n_row // 2
    inv = 1.0 / S
    row = lax.axis_index("row")
    col = lax.axis_index("col")
    chip = row // 2
    core = lax.rem(row, 2)
    sib = chip * 2 + 1 - core
    pending = []

    def send(c):
        c.start()
        pending.append(c)

    def other_row(d):
        return lax.rem(row + d, n_row)

    def other_col(d):
        return lax.rem(col + d, n_col)

    def other_chip(d):
        return lax.rem(chip + d, n_chip)

    barrier = pltpu.get_barrier_semaphore()
    for d in range(1, n_row):
        pl.semaphore_signal(barrier, inc=1, device_id={"row": other_row(d)}, device_id_type=MESH)
    for d in range(1, n_col):
        pl.semaphore_signal(barrier, inc=1, device_id={"col": other_col(d)}, device_id_type=MESH)

    g_copy = pltpu.make_async_copy(g_hbm, g_ref, g_sem)
    g_copy.start()

    wcat = jnp.concatenate([w1_ref[...], w2_ref[...]], axis=0)
    gamma = gamma_ref[...]
    wide = M // K
    x_all = x_ref[...].astype(F32).reshape(S * T, M)
    for a in range(wide):
        xs[a] = x_all[:, a * K:(a + 1) * K]
    for t in range(T):
        xt = jnp.concatenate([xs[a, pl.ds(t, S, stride=T), :] for a in range(wide)], axis=1)
        center = xt - jnp.mean(xt, axis=1, keepdims=True)
        rstd = lax.rsqrt(jnp.mean(center * center, axis=1, keepdims=True) + 1e-05)
        xhat = center * rstd
        normed = (xhat * gamma).astype(BF)
        xh[t] = xhat
        nm[t] = normed
        rs[t] = jnp.broadcast_to(rstd, (S, K))
        proj = mm_nt(wcat, normed)
        left[aligned(col * B + t * C, C, C), :] = proj[:C].astype(BF)
        rf[pl.ds(t, C, stride=T), :] = proj[C:]
    right_in[row] = rf[...].astype(BF)

    pl.semaphore_wait(barrier, n_row + n_col - 2)

    mine = aligned(col * B, B, B)
    for d in range(1, n_col):
        send(remote(left.at[mine], left.at[mine], lg_s.at[d], lg_r.at[col], col=other_col(d)))
    send(remote(right_in.at[row], right_in.at[row], rg_s.at[0], rg_r.at[row], row=sib))
    for d in range(1, n_chip):
        peer = other_chip(d) * 2 + core
        send(remote(right_in.at[row], right_in.at[row], rg_s.at[d], rg_r.at[row], row=peer))

    wf[...] = wo_ref[...].astype(F32)
    for e in range(C):
        wp[e * C:(e + 1) * C, :] = wf[pl.ds(e, C, stride=C), :].astype(BF)
    wpt[...] = wp[...].astype(F32).T.astype(BF)

    g_copy.wait()
    GN = 4 * J
    for n in range(I * J // GN):
        cols = slice(n * GN, (n + 1) * GN)
        g_out[:, cols] = mm_nt(wp[...], g_ref[cols, :]).astype(BF)

    for d in range(1, n_col):
        src = lax.rem(col + n_col - d, n_col)
        rows = aligned(src * B, B, B)
        remote(left.at[rows], left.at[rows], lg_s.at[d], lg_r.at[src], col=src).wait_recv()
    for k in range(I * C // S):
        left_t[:, k * S:(k + 1) * S] = left[k * S:(k + 1) * S, :].T

    for h in range(C // 2):
        rhs = jnp.concatenate([
            jnp.concatenate([
                g_out[(2 * h + a) * C:(2 * h + a + 1) * C, i * J:(i + 1) * J] for a in range(2)], axis=1)
            for i in range(I)], axis=0)
        acc = mm(left_t[...], rhs) * inv
        tiles = [acc[:, a * J:(a + 1) * J].T for a in range(2)]
        for q in range(n_row):
            blk = jnp.concatenate([t[q * T:(q + 1) * T] for t in tiles], axis=0)
            dr_out[q % 2, q // 2, h * 2 * T:(h + 1) * 2 * T, :] = blk.astype(BF)
    to_sib = remote(dr_out.at[1 - core], dr_sib, sib_s, sib_r, row=sib)
    send(to_sib)

    for d in range(1, n_chip):
        src = lax.rem(chip + n_chip - d, n_chip) * 2 + core
        remote(right_in.at[src], right_in.at[src], rg_s.at[d], rg_r.at[src], row=src).wait_recv()
        send(remote(right_in.at[src], right_in.at[src], rg_s.at[n_chip + d], rg_r.at[src], row=sib))
    remote(right_in.at[sib], right_in.at[sib], rg_s.at[0], rg_r.at[sib], row=sib).wait_recv()
    for d in range(1, n_chip):
        src = lax.rem(chip + n_chip - d, n_chip) * 2 + 1 - core
        remote(right_in.at[src], right_in.at[src], rg_s.at[0], rg_r.at[src], row=sib).wait_recv()

    def right_step(h, _):
        parts = [right_in[q, aligned(h * 2 * T, 2 * T, 2 * T), :].astype(F32) for q in range(n_row)]
        for a in range(2):
            tile = jnp.concatenate([p[a * T:(a + 1) * T] for p in parts], axis=0)
            right[aligned((2 * h + a) * J, J, J), :] = tile.astype(BF)
        return 0
    lax.fori_loop(0, C // 2, right_step, 0)

    to_sib.wait_recv()
    def pair_step(q, _):
        dr_sib[q] = (dr_out[core, q].astype(F32) + dr_sib[q].astype(F32)).astype(BF)
        return 0
    lax.fori_loop(0, n_chip, pair_step, 0)
    for d in range(1, n_chip):
        peer = other_chip(d)
        send(remote(dr_sib.at[peer], dr_in.at[chip], dr_s.at[d], dr_r.at[chip], row=peer * 2 + core))

    for k in range(n_col):
        owner = other_col(k + 1) if k < n_col - 1 else col
        lhs = jnp.concatenate([
            jnp.concatenate([
                g_out[e * C:(e + 1) * C, aligned((owner * T + t) * J, J, J)] for t in range(T)], axis=0)
            for e in range(C)], axis=1)
        dl_out[owner] = (mm(lhs, right[...]) * inv).astype(BF)
        if k < n_col - 1:
            send(remote(dl_out.at[owner], dl_in.at[col], dl_s.at[k], dl_r.at[col], col=owner))

    RB = I * C // 2
    NB = 4 * J
    for k in range(2):
        for n in range(C * J // NB):
            res = mm_nt(left[k * RB:(k + 1) * RB, :], right[n * NB:(n + 1) * NB, :])
            buf[k * RB:(k + 1) * RB, n * NB:(n + 1) * NB] = res.astype(BF)

    RW = CC // n_row
    DN = 4
    for h in range(DN):
        lhs = jnp.concatenate([
            jnp.concatenate([
                buf[i * C:(i + 1) * C, e * J:(e + 1) * J]
                for e in range(h * C // DN, (h + 1) * C // DN)], axis=0)
            for i in range(I)], axis=1)
        per = n_row // DN
        dw_out[h * per:(h + 1) * per] = mm(lhs, g_ref[...]).astype(BF).reshape(per, RW, K)
    for d in range(1, n_row):
        peer = other_row(d)
        send(remote(dw_out.at[peer], dw_in.at[row], w1_s.at[d], w1_r.at[row], row=peer))

    dl_sum = dl_out[col].astype(F32)
    for d in range(1, n_col):
        src = lax.rem(col + n_col - d, n_col)
        remote(dl_in.at[src], dl_in.at[src], dl_s.at[0], dl_r.at[src], col=src).wait_recv()
        dl_sum = dl_sum + dl_in[src].astype(F32)
    dl_own[...] = dl_sum.astype(BF)
    dr_sum = dr_sib[chip].astype(F32)
    for d in range(1, n_chip):
        src = lax.rem(chip + n_chip - d, n_chip)
        remote(dr_in.at[src], dr_in.at[src], dr_s.at[d], dr_r.at[src], row=src * 2 + core).wait_recv()
        dr_sum = dr_sum + dr_in[src].astype(F32)
    dr_own[...] = dr_sum

    gain = jnp.zeros((1, M), F32)
    wgrad = jnp.zeros((2 * C, M), F32)
    for t in range(T):
        dcat = jnp.concatenate(
            [dl_own[t * C:(t + 1) * C, :], dr_own[pl.ds(t, C, stride=T), :].astype(BF)], axis=0)
        wgrad = wgrad + mm(dcat, nm[t])
        dn = mm_tn(dcat, wcat)
        xhat = xh[t]
        gain = gain + jnp.sum(dn * xhat, axis=0, keepdims=True)
        hid = dn * gamma
        m1 = jnp.mean(hid, axis=1, keepdims=True)
        m2 = jnp.mean(hid * xhat, axis=1, keepdims=True)
        rstd = rs[t]
        rstd = jnp.concatenate([rstd] * wide, axis=1)
        grad = rstd * (hid - m1 - xhat * m2)
        for a in range(wide):
            xs[a, pl.ds(t, S, stride=T), :] = grad[:, a * K:(a + 1) * K]
    grads = jnp.concatenate([xs[a] for a in range(wide)], axis=1)
    ag_ref[...] = grads.reshape(S, T, M).astype(BF)

    RS = 2 * C * wide // n_row
    gain_rows = jnp.concatenate([gain[:, a * K:(a + 1) * K] for a in range(wide)]
                                + [jnp.zeros((8 - wide, K), F32)], axis=0)
    for q in range(n_row):
        a, r0 = divmod(q * RS, 2 * C)
        sm_out[q, 0:RS, :] = wgrad[r0:r0 + RS, a * K:(a + 1) * K]
        sm_out[q, RS:RS + 8, :] = gain_rows
    for d in range(1, n_row):
        peer = other_row(d)
        send(remote(sm_out.at[peer], sm_in.at[row], s1_s.at[d], s1_r.at[row], row=peer))

    def sum_row(own, got, ss, rr):
        total = own.astype(F32)
        for d in range(1, n_row):
            src = lax.rem(row + n_row - d, n_row)
            remote(got.at[src], got.at[src], ss.at[d], rr.at[src], row=src).wait_recv()
            total = total + got[src].astype(F32)
        return total

    def sum_col(own, got, ss, rr):
        total = own
        for d in range(1, n_col):
            src = lax.rem(col + n_col - d, n_col)
            remote(got.at[src], got.at[src], ss.at[d], rr.at[src], col=src).wait_recv()
            total = total + got[src]
        return total

    def z_step(p):
        rhs = jnp.concatenate([
            jnp.concatenate([
                buf[(2 * p + a) * C:(2 * p + a + 1) * C, e * J:(e + 1) * J] for e in range(C)], axis=0)
            for a in range(2)], axis=1)
        res = mm(wpt[...], rhs) * inv
        for a in range(2):
            z_buf[(2 * p + a) * J:(2 * p + a + 1) * J, :] = res[:, a * J:(a + 1) * J].T.astype(BF)

    z_copies = []
    def z_part(n, of):
        lo, hi = n * (I // 2) // of, (n + 1) * (I // 2) // of
        for p in range(lo, hi):
            z_step(p)
        rows = pl.ds(lo * 2 * J, (hi - lo) * 2 * J)
        c = pltpu.make_async_copy(z_buf.at[rows], z_hbm.at[rows], z_sem.at[n])
        c.start()
        z_copies.append(c)

    dw_blk[0] = sum_row(dw_out[row], dw_in, w1_s, w1_r)
    for d in range(1, n_col):
        send(remote(dw_blk.at[0], dw_col.at[col], w2_s.at[d], w2_r.at[col], col=other_col(d)))
    z_part(0, 4)
    sm_blk[...] = sum_row(sm_out[row], sm_in, s1_s, s1_r)
    for d in range(1, n_col):
        send(remote(sm_blk, sm_col.at[col], s2_s.at[d], s2_r.at[col], col=other_col(d)))
    z_part(1, 4)
    dw_blk[1] = sum_col(dw_blk[0], dw_col, w2_s, w2_r) * inv
    dw_full[row] = dw_blk[1]
    for d in range(1, n_row):
        send(remote(dw_blk.at[1], dw_full.at[row], w3_s.at[d], w3_r.at[row], row=other_row(d)))
    z_part(2, 4)
    sm_full[row] = sum_col(sm_blk[...], sm_col, s2_s, s2_r)
    for d in range(1, n_row):
        send(remote(sm_full.at[row], sm_full.at[row], s3_s.at[d], s3_r.at[row], row=other_row(d)))
    z_part(3, 4)

    for d in range(1, n_row):
        src = lax.rem(row + n_row - d, n_row)
        remote(dw_full.at[src], dw_full.at[src], w3_s.at[d], w3_r.at[src], row=src).wait_recv()
    for e in range(C):
        q, r0 = divmod(e * C, RW)
        dwo_ref[pl.ds(e, C, stride=C), :] = dw_full[q, r0:r0 + C, :]
    for d in range(1, n_row):
        src = lax.rem(row + n_row - d, n_row)
        remote(sm_full.at[src], sm_full.at[src], s3_s.at[d], s3_r.at[src], row=src).wait_recv()
    for q in range(n_row):
        a, r0 = divmod(q * RS, 2 * C)
        for out, lo in ((wl_ref, 0), (wr_ref, C)):
            if lo <= r0 < lo + C:
                out[r0 - lo:r0 - lo + RS, a * K:(a + 1) * K] = sm_full[q, 0:RS, :]
    for a in range(wide):
        gain_ref[:, a * K:(a + 1) * K] = sm_full[0, RS + a:RS + a + 1, :]

    for c in z_copies:
        c.wait()
    for c in pending:
        c.wait_send()


def on_device(n_row, n_col, x, gamma, w1, w2, wo, cot):
    S, T, M = x.shape
    C = w1.shape[1]
    CC, K = wo.shape
    I, J = cot.shape[0], cot.shape[1] * cot.shape[2]
    B = T * C
    n_chip = n_row // 2
    RW = CC // n_row
    RS = 2 * C * (M // K) // n_row
    V = lambda shape, dtype: pltpu.VMEM(shape, dtype)
    D = lambda n: pltpu.SemaphoreType.DMA((n,))
    vm = pl.BlockSpec(memory_space=pltpu.VMEM)
    hb = pl.BlockSpec(memory_space=pl.ANY)
    z, ag, wl, wr, dwo, gain = pl.pallas_call(
        functools.partial(kernel, n_row, n_col),
        out_shape=(
            jax.ShapeDtypeStruct((I * J, K), BF),
            jax.ShapeDtypeStruct((S, T, M), BF),
            jax.ShapeDtypeStruct((C, M), F32),
            jax.ShapeDtypeStruct((C, M), F32),
            jax.ShapeDtypeStruct((CC, K), F32),
            jax.ShapeDtypeStruct((1, M), F32),
        ),
        in_specs=[vm, vm, vm, vm, vm, hb],
        out_specs=(hb, vm, vm, vm, vm, vm),
        scratch_shapes=[
            V((I * J, K), BF),
            V((M // K, S * T, K), F32),
            V((T, S, M), F32),
            V((T, S, M), BF),
            V((T, S, K), F32),
            V((CC, K), BF),
            V((K, CC), BF),
            V((CC, K), F32),
            V((B, S), F32),
            V((n_row, B, S), BF),
            V((C * J, S), BF),
            V((I * C, S), BF),
            V((S, I * C), BF),
            V((CC, I * J), BF),
            V((I * C, C * J), BF),
            V((n_col, B, S), BF),
            V((n_col, B, S), BF),
            V((2, n_chip, B, S), BF),
            V((n_chip, B, S), BF),
            V((n_chip, B, S), BF),
            V((B, S), BF),
            V((B, S), F32),
            V((n_row, RW, K), BF),
            V((n_row, RW, K), BF),
            V((2, RW, K), F32),
            V((n_col, RW, K), F32),
            V((n_row, RW, K), F32),
            V((n_row, RS + 8, K), F32),
            V((n_row, RS + 8, K), F32),
            V((RS + 8, K), F32),
            V((n_col, RS + 8, K), F32),
            V((n_row, RS + 8, K), F32),
            V((I * J, K), BF),
            pltpu.SemaphoreType.DMA,
            D(4),
            D(n_row), D(n_row), D(n_col), D(n_col), D(n_col), D(n_col),
            pltpu.SemaphoreType.DMA, pltpu.SemaphoreType.DMA, D(n_chip), D(n_chip),
            D(n_row), D(n_row), D(n_col), D(n_col), D(n_row), D(n_row),
            D(n_row), D(n_row), D(n_col), D(n_col), D(n_row), D(n_row),
        ],
        compiler_params=pltpu.CompilerParams(
            collective_id=0, has_side_effects=True, vmem_limit_bytes=56 * 1024 * 1024,
        ),
    )(x, gamma.reshape(1, M), w1.T, w2.T, wo, cot.reshape(I * J, K))
    return z.reshape(cot.shape), ag, wl.T, wr.T, dwo, gain.reshape(M)


def solution(mesh):
    placed = (P(None, ("row", "col"), None), P(), P(), P(), P(), P("row", None, "col", None))
    return jax.shard_map(
        functools.partial(on_device, mesh.shape["row"], mesh.shape["col"]),
        mesh=mesh,
        in_specs=placed,
        out_specs=(P("row", None, "col", None), P(None, ("row", "col"), None), P(), P(), P(), P()),
        check_vma=False,
    )
```

```python
import functools

import jax
import jax.numpy as jnp
from jax import lax
from jax.experimental import pallas as pl
from jax.experimental.pallas import tpu as pltpu
from jax.sharding import PartitionSpec as P

MESH = pl.DeviceIdType.MESH
BF = jnp.bfloat16
F32 = jnp.float32
NT = (((1,), (1,)), ((), ()))
TN = (((0,), (0,)), ((), ()))


def mm(a, b):
    return jnp.dot(a, b, preferred_element_type=F32)


def mm_nt(a, b):
    return lax.dot_general(a, b, NT, preferred_element_type=F32)


def mm_tn(a, b):
    return lax.dot_general(a, b, TN, preferred_element_type=F32)


def remote(src, dst, send_sem, recv_sem, **where):
    return pltpu.make_async_remote_copy(
        src_ref=src, dst_ref=dst, send_sem=send_sem, recv_sem=recv_sem,
        device_id=where, device_id_type=MESH,
    )


def aligned(start, size, multiple):
    return pl.ds(pl.multiple_of(start, multiple), size)


def kernel(
    n_row, n_col,
    x_ref, gamma_ref, w1_ref, w2_ref, wo_ref, g_hbm,
    z_hbm, ag_hbm, wl_ref, wr_ref, dwo_ref, gain_ref,
    g_ref, xs, xh, nm, rs, wp, wpt, wf, rf, right_in, right, left, left_t, g_out, buf,
    dl_out, dl_in, dr_out, dr_sib, dr_in, dl_own, dr_own,
    dw_give, dw_sib, dw_own, dw_pair, dw_in, dw_blk, dw_chip, dw_full,
    sm_give, sm_sib, sm_own, sm_col, sm_sum, sm_chip, sm_half, z_buf, ag_buf,
    g_sem, z_sem, ag_sem, rg_s, rg_r, lg_s, lg_r, dl_s, dl_r, dr_s, dr_r,
    d1_s, d1_r, d2_s, d2_r, d3_s, d3_r, d4_s, d4_r, d5_s, d5_r,
    s1_s, s1_r, s2_s, s2_r, s3_s, s3_r, s4_s, s4_r,
):
    S, T, M = x_ref.shape
    C = w1_ref.shape[0]
    CC, K = wo_ref.shape
    J = n_row * T
    I = n_col * T
    B = T * C
    n_chip = n_row // 2
    inv = 1.0 / S
    row = lax.axis_index("row")
    col = lax.axis_index("col")
    chip = row // 2
    core = lax.rem(row, 2)
    sib = chip * 2 + 1 - core
    n_x, n_y = n_row // 4, n_col // 2
    x, zh = row // 4, lax.rem(row, 4) // 2
    zl, y = col // n_y, lax.rem(col, n_y)

    def row_of(dx, far, other):
        z = 1 - zh if far else zh
        return lax.rem(x + dx, n_x) * 4 + z * 2 + (1 - core if other else core)

    def col_of(dy, far):
        return (1 - zl if far else zl) * n_y + lax.rem(y + dy, n_y)

    pending = []

    def send(c):
        c.start()
        pending.append(c)

    def other_col(d):
        return lax.rem(col + d, n_col)

    def other_chip(d):
        return lax.rem(chip + d, n_chip)

    barrier = pltpu.get_barrier_semaphore()
    pl.semaphore_signal(barrier, inc=1, device_id={"row": sib}, device_id_type=MESH)
    for d in range(1, n_chip):
        peer = other_chip(d) * 2 + core
        pl.semaphore_signal(barrier, inc=1, device_id={"row": peer}, device_id_type=MESH)
    for d in range(1, n_col):
        pl.semaphore_signal(barrier, inc=1, device_id={"col": other_col(d)}, device_id_type=MESH)

    g_copy = pltpu.make_async_copy(g_hbm, g_ref, g_sem)
    g_copy.start()

    wcat = jnp.concatenate([w1_ref[...], w2_ref[...]], axis=0)
    gamma = gamma_ref[...]
    wide = M // K
    x_all = x_ref[...].astype(F32).reshape(S * T, M)
    for a in range(wide):
        xs[a] = x_all[:, a * K:(a + 1) * K]
    for t in range(T):
        xt = jnp.concatenate([xs[a, pl.ds(t, S, stride=T), :] for a in range(wide)], axis=1)
        center = xt - jnp.mean(xt, axis=1, keepdims=True)
        rstd = lax.rsqrt(jnp.mean(center * center, axis=1, keepdims=True) + 1e-05)
        xhat = center * rstd
        normed = (xhat * gamma).astype(BF)
        xh[t] = xhat
        nm[t] = normed
        rs[t] = jnp.broadcast_to(rstd, (S, K))
        proj = mm_nt(wcat, normed)
        left[aligned(col * B + t * C, C, C), :] = proj[:C].astype(BF)
        rf[pl.ds(t, C, stride=T), :] = proj[C:]
    right_in[row] = rf[...].astype(BF)

    pl.semaphore_wait(barrier, n_chip + n_col - 1)

    def left_rows(c):
        return aligned(c * B, B, B)

    def send_right(block, slot, to):
        send(remote(right_in.at[block], right_in.at[block], rg_s.at[slot], rg_r.at[block], row=to))

    def wait_right(block):
        remote(right_in.at[block], right_in.at[block], rg_s.at[0], rg_r.at[block], row=sib).wait_recv()

    def send_left(block, slot, to):
        rows = left_rows(block)
        send(remote(left.at[rows], left.at[rows], lg_s.at[slot], lg_r.at[block], col=to))

    def wait_left(block):
        rows = left_rows(block)
        remote(left.at[rows], left.at[rows], lg_s.at[0], lg_r.at[block], col=col_of(0, True)).wait_recv()

    send_right(row, 0, row_of(0, True, False))
    send_left(col, 0, col_of(0, True))
    for d in range(1, n_x):
        send_right(row, d, row_of(d, False, False))
    for d in range(1, n_y):
        send_left(col, d, col_of(d, False))
    send_right(row, 2 * n_x, sib)

    wf[...] = wo_ref[...].astype(F32)
    for e in range(C):
        wp[e * C:(e + 1) * C, :] = wf[pl.ds(e, C, stride=C), :].astype(BF)
    wpt[...] = wp[...].astype(F32).T.astype(BF)

    g_copy.wait()
    GN = 4 * J

    def g_outer_part(lo, hi):
        for n in range(lo, hi):
            cols = slice(n * GN, (n + 1) * GN)
            g_out[:, cols] = mm_nt(wp[...], g_ref[cols, :]).astype(BF)

    n_go = I * J // GN
    g_outer_part(0, n_go // 2)

    far_row, far_col = row_of(0, True, False), col_of(0, True)
    wait_right(far_row)
    for d in range(1, n_x):
        send_right(far_row, n_x + d, row_of(d, False, False))
    send_right(far_row, n_x, sib)
    wait_left(far_col)
    for d in range(1, n_y):
        send_left(far_col, n_y + d, col_of(d, False))

    g_outer_part(n_go // 2, n_go)

    for d in range(1, n_x):
        block = row_of(d, False, False)
        wait_right(block)
        send_right(block, 2 * n_x + d, sib)
    for d in range(1, n_y):
        wait_left(col_of(d, False))
    for d in range(1, n_y):
        wait_left(col_of(d, True))
    for d in range(1, n_x):
        block = row_of(d, True, False)
        wait_right(block)
        send_right(block, 3 * n_x + d, sib)
    for k in range(I * C // S):
        left_t[:, k * S:(k + 1) * S] = left[k * S:(k + 1) * S, :].T

    for h in range(C // 2):
        rhs = jnp.concatenate([
            jnp.concatenate([
                g_out[(2 * h + a) * C:(2 * h + a + 1) * C, i * J:(i + 1) * J] for a in range(2)], axis=1)
            for i in range(I)], axis=0)
        acc = mm(left_t[...], rhs) * inv
        tiles = [acc[:, a * J:(a + 1) * J].T for a in range(2)]
        for q in range(n_row):
            blk = jnp.concatenate([t[q * T:(q + 1) * T] for t in tiles], axis=0)
            dr_out[q % 2, q // 2, h * 2 * T:(h + 1) * 2 * T, :] = blk.astype(BF)
    to_sib = remote(dr_out.at[1 - core], dr_sib, dr_s.at[0], dr_r.at[n_chip], row=sib)
    send(to_sib)

    for far in (False, True):
        for d in range(n_x):
            wait_right(row_of(d, far, True))
    def right_step(h, _):
        parts = [right_in[q, aligned(h * 2 * T, 2 * T, 2 * T), :].astype(F32) for q in range(n_row)]
        for a in range(2):
            tile = jnp.concatenate([p[a * T:(a + 1) * T] for p in parts], axis=0)
            right[aligned((2 * h + a) * J, J, J), :] = tile.astype(BF)
        return 0
    lax.fori_loop(0, C // 2, right_step, 0)

    def right_grad_out():
        to_sib.wait_recv()
        def pair_step(q, _):
            dr_sib[q] = (dr_out[core, q].astype(F32) + dr_sib[q].astype(F32)).astype(BF)
            return 0
        lax.fori_loop(0, n_chip, pair_step, 0)
        for d in range(1, n_chip):
            peer = other_chip(d)
            send(remote(dr_sib.at[peer], dr_in.at[chip], dr_s.at[d], dr_r.at[chip], row=peer * 2 + core))

    for k in range(n_col):
        owner = other_col(k + 1) if k < n_col - 1 else col
        lhs = jnp.concatenate([
            jnp.concatenate([
                g_out[e * C:(e + 1) * C, aligned((owner * T + t) * J, J, J)] for t in range(T)], axis=0)
            for e in range(C)], axis=1)
        dl_out[owner] = (mm(lhs, right[...]) * inv).astype(BF)
        if k == n_col // 2 - 1:
            right_grad_out()
        if k < n_col - 1:
            send(remote(dl_out.at[owner], dl_in.at[col], dl_s.at[k], dl_r.at[col], col=owner))

    RB = I * C // 2
    NB = 4 * J
    for k in range(2):
        for n in range(C * J // NB):
            res = mm_nt(left[k * RB:(k + 1) * RB, :], right[n * NB:(n + 1) * NB, :])
            buf[k * RB:(k + 1) * RB, n * NB:(n + 1) * NB] = res.astype(BF)

    HW = CC // 2
    QE = C // 4

    def dw_quarter(e0):
        lhs = jnp.concatenate([
            jnp.concatenate([
                buf[i * C:(i + 1) * C, aligned((e0 + e) * J, J, J)] for e in range(QE)], axis=0)
            for i in range(I)], axis=1)
        return mm(lhs, g_ref[...])

    for q in range(2):
        rows = slice(q * HW // 2, (q + 1) * HW // 2)
        dw_give[rows, :] = dw_quarter((1 - core) * 2 * QE + q * QE).astype(BF)
    dw_to_sib = remote(dw_give, dw_sib, d1_s, d1_r, row=sib)
    send(dw_to_sib)
    for q in range(2):
        rows = slice(q * HW // 2, (q + 1) * HW // 2)
        dw_own[rows, :] = dw_quarter(core * 2 * QE + q * QE)

    RW = HW // n_col
    dw_to_sib.wait_recv()
    dw_pair[...] = (dw_own[...] + dw_sib[...].astype(F32)).astype(BF).reshape(n_col, RW, K)
    for d in range(1, n_col):
        peer = other_col(d)
        send(remote(dw_pair.at[peer], dw_in.at[col], d2_s.at[d], d2_r.at[col], col=peer))

    dl_sum = dl_out[col].astype(F32)
    for d in range(1, n_col):
        src = lax.rem(col + n_col - d, n_col)
        remote(dl_in.at[src], dl_in.at[src], dl_s.at[0], dl_r.at[src], col=src).wait_recv()
        dl_sum = dl_sum + dl_in[src].astype(F32)
    dl_own[...] = dl_sum.astype(BF)
    dr_sum = dr_sib[chip].astype(F32)
    for d in range(1, n_chip):
        src = lax.rem(chip + n_chip - d, n_chip)
        remote(dr_in.at[src], dr_in.at[src], dr_s.at[d], dr_r.at[src], row=src * 2 + core).wait_recv()
        dr_sum = dr_sum + dr_in[src].astype(F32)
    dr_own[...] = dr_sum

    gain = jnp.zeros((1, M), F32)
    wgrad = jnp.zeros((2 * C, M), F32)
    for t in range(T):
        dcat = jnp.concatenate(
            [dl_own[t * C:(t + 1) * C, :], dr_own[pl.ds(t, C, stride=T), :].astype(BF)], axis=0)
        wgrad = wgrad + mm(dcat, nm[t])
        dn = mm_tn(dcat, wcat)
        xhat = xh[t]
        gain = gain + jnp.sum(dn * xhat, axis=0, keepdims=True)
        hid = dn * gamma
        m1 = jnp.mean(hid, axis=1, keepdims=True)
        m2 = jnp.mean(hid * xhat, axis=1, keepdims=True)
        rstd = rs[t]
        rstd = jnp.concatenate([rstd] * wide, axis=1)
        grad = rstd * (hid - m1 - xhat * m2)
        for a in range(wide):
            xs[a, pl.ds(t, S, stride=T), :] = grad[:, a * K:(a + 1) * K]
    grads = jnp.concatenate([xs[a] for a in range(wide)], axis=1)
    ag_buf[...] = grads.reshape(S, T, M).astype(BF)
    ag_copy = pltpu.make_async_copy(ag_buf, ag_hbm, ag_sem)
    ag_copy.start()

    RS = 2 * C
    for a in range(wide):
        sm_own[a, 0:RS, :] = wgrad[:, a * K:(a + 1) * K]
        sm_own[a, RS:RS + 8, :] = jnp.broadcast_to(gain[:, a * K:(a + 1) * K], (8, K))
    sm_to_sib = remote(sm_own.at[1 - core], sm_sib, s1_s, s1_r, row=sib)
    send(sm_to_sib)

    def sum_chips(own, got, ss, rr):
        total = own
        for d in range(1, n_chip):
            src = lax.rem(chip + n_chip - d, n_chip)
            remote(got.at[src], got.at[src], ss.at[d], rr.at[src], row=src * 2 + core).wait_recv()
            total = total + got[src].astype(F32)
        return total

    def sum_cols(own, got, ss, rr):
        total = own
        for d in range(1, n_col):
            src = lax.rem(col + n_col - d, n_col)
            remote(got.at[src], got.at[src], ss.at[d], rr.at[src], col=src).wait_recv()
            total = total + got[src].astype(F32)
        return total

    def to_chips(src, dst, ss, rr):
        for d in range(1, n_chip):
            peer = other_chip(d) * 2 + core
            send(remote(src, dst.at[chip], ss.at[d], rr.at[chip], row=peer))

    def to_cols(src, dst, ss, rr):
        for d in range(1, n_col):
            send(remote(src, dst.at[col], ss.at[d], rr.at[col], col=other_col(d)))

    def z_step(p):
        rhs = jnp.concatenate([
            jnp.concatenate([
                buf[(2 * p + a) * C:(2 * p + a + 1) * C, e * J:(e + 1) * J] for e in range(C)], axis=0)
            for a in range(2)], axis=1)
        res = mm(wpt[...], rhs) * inv
        for a in range(2):
            z_buf[(2 * p + a) * J:(2 * p + a + 1) * J, :] = res[:, a * J:(a + 1) * J].T.astype(BF)

    z_copies = []
    def z_part(n, of):
        lo, hi = n * (I // 2) // of, (n + 1) * (I // 2) // of
        for p in range(lo, hi):
            z_step(p)
        rows = pl.ds(lo * 2 * J, (hi - lo) * 2 * J)
        c = pltpu.make_async_copy(z_buf.at[rows], z_hbm.at[rows], z_sem.at[n])
        c.start()
        z_copies.append(c)

    z_part(0, 4)
    sm_to_sib.wait_recv()
    sm_give[...] = sm_own[core] + sm_sib[...]
    to_cols(sm_give, sm_col, s2_s, s2_r)
    z_part(1, 4)
    own = dw_pair[col].astype(F32)
    dw_blk[0] = sum_cols(own, dw_in, d2_s, d2_r).astype(BF)
    to_chips(dw_blk.at[0], dw_chip, d3_s, d3_r)
    z_part(2, 4)
    sm_sum[...] = sum_cols(sm_give[...], sm_col, s2_s, s2_r)
    to_chips(sm_sum, sm_chip, s3_s, s3_r)
    z_part(3, 4)
    dw_blk[1] = (sum_chips(dw_blk[0].astype(F32), dw_chip, d3_s, d3_r) * inv).astype(BF)
    to_cols(dw_blk.at[1], dw_full.at[core], d4_s, d4_r)
    dw_full[core, col] = dw_blk[1]
    sm_half[core] = sum_chips(sm_sum[...], sm_chip, s3_s, s3_r)
    sm_back = remote(sm_half.at[core], sm_half.at[core], s4_s, s4_r.at[core], row=sib)
    send(sm_back)
    for d in range(1, n_col):
        src = lax.rem(col + n_col - d, n_col)
        got = dw_full.at[core, src]
        remote(got, got, d4_s.at[d], d4_r.at[src], col=src).wait_recv()
    send(remote(dw_full.at[core], dw_full.at[core], d5_s, d5_r.at[core], row=sib))

    def put_dw(h):
        per = RW // C
        for e in range(C // 2):
            part = dw_full[h, e // per].astype(F32)
            dwo_ref[pl.ds(h * (C // 2) + e, C, stride=C), :] = part[(e % per) * C:(e % per + 1) * C]

    got = sm_half.at[1 - core]
    remote(got, got, s4_s, s4_r.at[1 - core], row=sib).wait_recv()
    for a in range(wide):
        lanes = slice(a * K, (a + 1) * K)
        wl_ref[:, lanes] = sm_half[a, 0:C, :]
        wr_ref[:, lanes] = sm_half[a, C:2 * C, :]
        gain_ref[:, lanes] = sm_half[a, RS:RS + 1, :]
    got = dw_full.at[1 - core]
    remote(got, got, d5_s, d5_r.at[1 - core], row=sib).wait_recv()
    put_dw(0)
    put_dw(1)

    ag_copy.wait()
    for c in z_copies:
        c.wait()
    for c in pending:
        c.wait_send()


def settle_kernel(*refs):
    n = (len(refs) - 2) // 3
    srcs, dsts, held = refs[:n], refs[n:2 * n], refs[2 * n:3 * n]
    in_sems, out_sems = refs[3 * n:]
    loads, stores = [], []
    for src, dst, mid in zip(srcs, dsts, held):
        parts = 4 if src.shape[0] >= 4096 else 1
        rows = src.shape[0] // parts
        for p in range(parts):
            part = pl.ds(p * rows, rows)
            k = len(loads)
            loads.append(pltpu.make_async_copy(src.at[part], mid.at[part], in_sems.at[k]))
            stores.append(pltpu.make_async_copy(mid.at[part], dst.at[part], out_sems.at[k]))
            loads[-1].start()
    for load, store in zip(loads, stores):
        load.wait()
        store.start()
    for store in stores:
        store.wait()


def settle(arrays):
    hb = pl.BlockSpec(memory_space=pl.ANY)
    sems = pltpu.SemaphoreType.DMA((len(arrays) + 3,))
    return pl.pallas_call(
        settle_kernel,
        out_shape=tuple(jax.ShapeDtypeStruct(a.shape, a.dtype) for a in arrays),
        in_specs=[hb] * len(arrays),
        out_specs=(hb,) * len(arrays),
        scratch_shapes=[pltpu.VMEM(a.shape, a.dtype) for a in arrays] + [sems, sems],
        compiler_params=pltpu.CompilerParams(vmem_limit_bytes=62 * 1024 * 1024),
    )(*arrays)


def on_device(n_row, n_col, x, gamma, w1, w2, wo, cot):
    S, T, M = x.shape
    C = w1.shape[1]
    CC, K = wo.shape
    I, J = cot.shape[0], cot.shape[1] * cot.shape[2]
    B = T * C
    n_chip = n_row // 2
    RW = CC // 2 // n_col
    RS = 2 * C + 8
    one = pltpu.SemaphoreType.DMA
    V = lambda shape, dtype: pltpu.VMEM(shape, dtype)
    D = lambda n: pltpu.SemaphoreType.DMA((n,))
    vm = pl.BlockSpec(memory_space=pltpu.VMEM)
    hb = pl.BlockSpec(memory_space=pl.ANY)
    z, ag, wl, wr, dwo, gain = pl.pallas_call(
        functools.partial(kernel, n_row, n_col),
        out_shape=(
            jax.ShapeDtypeStruct((I * J, K), BF),
            jax.ShapeDtypeStruct((S, T, M), BF),
            jax.ShapeDtypeStruct((C, M), F32),
            jax.ShapeDtypeStruct((C, M), F32),
            jax.ShapeDtypeStruct((CC, K), F32),
            jax.ShapeDtypeStruct((1, M), F32),
        ),
        in_specs=[vm, vm, vm, vm, vm, hb],
        out_specs=(hb, hb, vm, vm, vm, vm),
        scratch_shapes=[
            V((I * J, K), BF),
            V((M // K, S * T, K), F32),
            V((T, S, M), F32),
            V((T, S, M), BF),
            V((T, S, K), F32),
            V((CC, K), BF),
            V((K, CC), BF),
            V((CC, K), F32),
            V((B, S), F32),
            V((n_row, B, S), BF),
            V((C * J, S), BF),
            V((I * C, S), BF),
            V((S, I * C), BF),
            V((CC, I * J), BF),
            V((I * C, C * J), BF),
            V((n_col, B, S), BF),
            V((n_col, B, S), BF),
            V((2, n_chip, B, S), BF),
            V((n_chip, B, S), BF),
            V((n_chip, B, S), BF),
            V((B, S), BF),
            V((B, S), F32),
            V((CC // 2, K), BF),
            V((CC // 2, K), BF),
            V((CC // 2, K), F32),
            V((n_col, RW, K), BF),
            V((n_col, RW, K), BF),
            V((2, RW, K), BF),
            V((n_chip, RW, K), BF),
            V((2, n_col, RW, K), BF),
            V((RS, K), F32),
            V((RS, K), F32),
            V((2, RS, K), F32),
            V((n_col, RS, K), F32),
            V((RS, K), F32),
            V((n_chip, RS, K), F32),
            V((2, RS, K), F32),
            V((I * J, K), BF),
            V((S, T, M), BF),
            one, D(4), one,
            D(n_row), D(n_row), D(n_col), D(n_col), D(n_col), D(n_col), D(n_chip), D(n_chip + 1),
            one, one, D(n_col), D(n_col), D(n_chip), D(n_chip), D(n_col), D(n_col), one, D(2),
            one, one, D(n_col), D(n_col), D(n_chip), D(n_chip), one, D(2),
        ],
        compiler_params=pltpu.CompilerParams(
            collective_id=0, has_side_effects=True, vmem_limit_bytes=56 * 1024 * 1024,
        ),
    )(x, gamma.reshape(1, M), w1.T, w2.T, wo, cot.reshape(I * J, K))
    z, ag, wl, wr, dwo, gain = settle((z, ag, wl, wr, dwo, gain))
    return z.reshape(cot.shape), ag, wl.T, wr.T, dwo, gain.reshape(M)


def solution(mesh):
    placed = (P(None, ("row", "col"), None), P(), P(), P(), P(), P("row", None, "col", None))
    return jax.shard_map(
        functools.partial(on_device, mesh.shape["row"], mesh.shape["col"]),
        mesh=mesh,
        in_specs=placed,
        out_specs=(P("row", None, "col", None), P(None, ("row", "col"), None), P(), P(), P(), P()),
        check_vma=False,
    )
```

```python
import functools

import jax
import jax.numpy as jnp
from jax import lax
from jax.experimental import pallas as pl
from jax.experimental.pallas import tpu as pltpu
from jax.sharding import PartitionSpec as P

MESH = pl.DeviceIdType.MESH
BF = jnp.bfloat16
F32 = jnp.float32
NT = (((1,), (1,)), ((), ()))
TN = (((0,), (0,)), ((), ()))


def mm(a, b):
    return jnp.dot(a, b, preferred_element_type=F32)


def mm_nt(a, b):
    return lax.dot_general(a, b, NT, preferred_element_type=F32)


def mm_tn(a, b):
    return lax.dot_general(a, b, TN, preferred_element_type=F32)


def remote(src, dst, send_sem, recv_sem, **where):
    return pltpu.make_async_remote_copy(
        src_ref=src, dst_ref=dst, send_sem=send_sem, recv_sem=recv_sem,
        device_id=where, device_id_type=MESH,
    )


def aligned(start, size, multiple):
    return pl.ds(pl.multiple_of(start, multiple), size)


def kernel(
    n_row, n_col,
    x_ref, gamma_ref, w1_ref, w2_ref, wo_ref, g_hbm,
    z_hbm, ag_hbm, wl_ref, wr_ref, dwo_ref, gain_ref,
    g_ref, xs, xh, nm, rs, wp, wpt, wf, rf, right_in, right, left, left_t, g_out, buf,
    dl_out, dl_in, dr_acc, dr_out, dr_sib, dr_in, dl_own, dr_own,
    dw_give, dw_sib, dw_own, dw_pair, dw_in, dw_blk, dw_chip, dw_full,
    sm_give, sm_sib, sm_own, sm_out, sm_col, sm_sum, sm_chip, sm_half, z_buf, ag_buf,
    g_sem, z_sem, ag_sem, rg_s, rg_r, lg_s, lg_r, dl_s, dl_r, dr_s, dr_r,
    d1_s, d1_r, d2_s, d2_r, d3_s, d3_r, d4_s, d4_r, d5_s, d5_r,
    s1_s, s1_r, s2_s, s2_r, s3_s, s3_r, s4_s, s4_r,
):
    S, T, M = x_ref.shape
    C = w1_ref.shape[0]
    CC, K = wo_ref.shape
    J = n_row * T
    I = n_col * T
    B = T * C
    n_chip = n_row // 2
    inv = 1.0 / S
    row = lax.axis_index("row")
    col = lax.axis_index("col")
    chip = row // 2
    core = lax.rem(row, 2)
    sib = chip * 2 + 1 - core
    n_x, n_y = n_row // 4, n_col // 2
    x, zh = row // 4, lax.rem(row, 4) // 2
    zl, y = col // n_y, lax.rem(col, n_y)

    def row_of(dx, far, other):
        z = 1 - zh if far else zh
        return lax.rem(x + dx, n_x) * 4 + z * 2 + (1 - core if other else core)

    def col_of(dy, far):
        return (1 - zl if far else zl) * n_y + lax.rem(y + dy, n_y)

    pending = []

    def send(c):
        c.start()
        pending.append(c)

    def other_col(d):
        return lax.rem(col + d, n_col)

    def other_chip(d):
        return lax.rem(chip + d, n_chip)

    barrier = pltpu.get_barrier_semaphore()
    pl.semaphore_signal(barrier, inc=1, device_id={"row": sib}, device_id_type=MESH)
    for d in range(1, n_chip):
        peer = other_chip(d) * 2 + core
        pl.semaphore_signal(barrier, inc=1, device_id={"row": peer}, device_id_type=MESH)
    for d in range(1, n_col):
        pl.semaphore_signal(barrier, inc=1, device_id={"col": other_col(d)}, device_id_type=MESH)

    g_copy = pltpu.make_async_copy(g_hbm, g_ref, g_sem)
    g_copy.start()

    wcat = jnp.concatenate([w1_ref[...], w2_ref[...]], axis=0)
    gamma = gamma_ref[...]
    wide = M // K
    x_all = x_ref[...].astype(F32).reshape(S * T, M)
    for a in range(wide):
        xs[a] = x_all[:, a * K:(a + 1) * K]
    for t in range(T):
        xt = jnp.concatenate([xs[a, pl.ds(t, S, stride=T), :] for a in range(wide)], axis=1)
        center = xt - jnp.mean(xt, axis=1, keepdims=True)
        rstd = lax.rsqrt(jnp.mean(center * center, axis=1, keepdims=True) + 1e-05)
        xhat = center * rstd
        normed = (xhat * gamma).astype(BF)
        xh[t] = xhat
        nm[t] = normed
        rs[t] = jnp.broadcast_to(rstd, (S, K))
        proj = mm_nt(wcat, normed)
        left[aligned(col * B + t * C, C, C), :] = proj[:C].astype(BF)
        rf[pl.ds(t, C, stride=T), :] = proj[C:]
    right_in[row] = rf[...].astype(BF)

    pl.semaphore_wait(barrier, n_chip + n_col - 1)

    def left_rows(c):
        return aligned(c * B, B, B)

    def send_right(block, slot, to):
        send(remote(right_in.at[block], right_in.at[block], rg_s.at[slot], rg_r.at[block], row=to))

    def wait_right(block):
        remote(right_in.at[block], right_in.at[block], rg_s.at[0], rg_r.at[block], row=sib).wait_recv()

    def send_left(block, slot, to):
        rows = left_rows(block)
        send(remote(left.at[rows], left.at[rows], lg_s.at[slot], lg_r.at[block], col=to))

    def wait_left(block):
        rows = left_rows(block)
        remote(left.at[rows], left.at[rows], lg_s.at[0], lg_r.at[block], col=col_of(0, True)).wait_recv()

    send_right(row, 0, row_of(0, True, False))
    send_left(col, 0, col_of(0, True))
    for d in range(1, n_x):
        send_right(row, d, row_of(d, False, False))
    for d in range(1, n_y):
        send_left(col, d, col_of(d, False))
    send_right(row, 2 * n_x, sib)

    wf[...] = wo_ref[...].astype(F32)
    for e in range(C):
        wp[e * C:(e + 1) * C, :] = wf[pl.ds(e, C, stride=C), :].astype(BF)
    wpt[...] = wp[...].astype(F32).T.astype(BF)

    g_copy.wait()
    GN = 4 * J

    def g_outer_part(lo, hi):
        for n in range(lo, hi):
            cols = slice(n * GN, (n + 1) * GN)
            g_out[:, cols] = mm_nt(wp[...], g_ref[cols, :]).astype(BF)

    n_go = I * J // GN
    g_outer_part(0, n_go // 2)

    far_row, far_col = row_of(0, True, False), col_of(0, True)
    wait_right(far_row)
    for d in range(1, n_x):
        send_right(far_row, n_x + d, row_of(d, False, False))
    send_right(far_row, n_x, sib)
    wait_left(far_col)
    for d in range(1, n_y):
        send_left(far_col, n_y + d, col_of(d, False))

    g_outer_part(n_go // 2, n_go)

    HB = n_col // 2 * B
    HI = I // 2

    def turn_left(z, h):
        for k in range(HB // S):
            left_t[h, :, k * S:(k + 1) * S] = left[aligned(z * HB + k * S, S, S), :].T

    def right_grad(z, h, p):
        rhs = jnp.concatenate([
            jnp.concatenate([
                g_out[(2 * p + a) * C:(2 * p + a + 1) * C, aligned((z * HI + i) * J, J, J)]
                for a in range(2)], axis=1)
            for i in range(HI)], axis=0)
        return mm(left_t[h], rhs)

    for d in range(1, n_y):
        wait_left(col_of(d, False))
    turn_left(zl, 0)
    for p in range(C // 2):
        dr_acc[:, 2 * p * J:(2 * p + 2) * J] = right_grad(zl, 0, p)

    for d in range(1, n_x):
        block = row_of(d, False, False)
        wait_right(block)
        send_right(block, 2 * n_x + d, sib)
    for d in range(1, n_y):
        wait_left(col_of(d, True))
    turn_left(1 - zl, 1)
    for p in range(C // 2):
        if p == C // 8:
            for d in range(1, n_x):
                block = row_of(d, True, False)
                wait_right(block)
                send_right(block, 3 * n_x + d, sib)
        acc = (dr_acc[:, 2 * p * J:(2 * p + 2) * J] + right_grad(1 - zl, 1, p)) * inv
        tiles = [acc[:, a * J:(a + 1) * J].T for a in range(2)]
        for q in range(n_row):
            blk = jnp.concatenate([t[q * T:(q + 1) * T] for t in tiles], axis=0)
            dr_out[q % 2, q // 2, p * 2 * T:(p + 1) * 2 * T, :] = blk.astype(BF)
    to_sib = remote(dr_out.at[1 - core], dr_sib, dr_s.at[0], dr_r.at[n_chip], row=sib)
    send(to_sib)

    for far in (False, True):
        for d in range(n_x):
            wait_right(row_of(d, far, True))
    def right_step(h, _):
        parts = [right_in[q, aligned(h * 2 * T, 2 * T, 2 * T), :].astype(F32) for q in range(n_row)]
        for a in range(2):
            tile = jnp.concatenate([p[a * T:(a + 1) * T] for p in parts], axis=0)
            right[aligned((2 * h + a) * J, J, J), :] = tile.astype(BF)
        return 0
    lax.fori_loop(0, C // 2, right_step, 0)

    def right_grad_out():
        to_sib.wait_recv()
        def pair_step(q, _):
            dr_sib[q] = (dr_out[core, q].astype(F32) + dr_sib[q].astype(F32)).astype(BF)
            return 0
        lax.fori_loop(0, n_chip, pair_step, 0)
        for d in range(1, n_chip):
            peer = other_chip(d)
            send(remote(dr_sib.at[peer], dr_in.at[chip], dr_s.at[d], dr_r.at[chip], row=peer * 2 + core))

    for k in range(n_col):
        owner = other_col(k + 1) if k < n_col - 1 else col
        lhs = jnp.concatenate([
            jnp.concatenate([
                g_out[e * C:(e + 1) * C, aligned((owner * T + t) * J, J, J)] for t in range(T)], axis=0)
            for e in range(C)], axis=1)
        dl_out[owner] = (mm(lhs, right[...]) * inv).astype(BF)
        if k == n_col // 2 - 1:
            right_grad_out()
        if k < n_col - 1:
            send(remote(dl_out.at[owner], dl_in.at[col], dl_s.at[k], dl_r.at[col], col=owner))

    RB = I * C // 2
    NB = 4 * J
    for k in range(2):
        for n in range(C * J // NB):
            res = mm_nt(left[k * RB:(k + 1) * RB, :], right[n * NB:(n + 1) * NB, :])
            buf[k * RB:(k + 1) * RB, n * NB:(n + 1) * NB] = res.astype(BF)

    HW = CC // 2
    QE = C // 4

    def dw_quarter(e0):
        lhs = jnp.concatenate([
            jnp.concatenate([
                buf[i * C:(i + 1) * C, aligned((e0 + e) * J, J, J)] for e in range(QE)], axis=0)
            for i in range(I)], axis=1)
        return mm(lhs, g_ref[...])

    for q in range(2):
        rows = slice(q * HW // 2, (q + 1) * HW // 2)
        dw_give[rows, :] = dw_quarter((1 - core) * 2 * QE + q * QE).astype(BF)
    dw_to_sib = remote(dw_give, dw_sib, d1_s, d1_r, row=sib)
    send(dw_to_sib)
    for q in range(2):
        rows = slice(q * HW // 2, (q + 1) * HW // 2)
        dw_own[rows, :] = dw_quarter(core * 2 * QE + q * QE)

    RW = HW // n_col
    dw_to_sib.wait_recv()
    dw_pair[...] = (dw_own[...] + dw_sib[...].astype(F32)).astype(BF).reshape(n_col, RW, K)
    for d in range(1, n_col):
        peer = other_col(d)
        send(remote(dw_pair.at[peer], dw_in.at[col], d2_s.at[d], d2_r.at[col], col=peer))

    dl_sum = dl_out[col].astype(F32)
    for d in range(1, n_col):
        src = lax.rem(col + n_col - d, n_col)
        remote(dl_in.at[src], dl_in.at[src], dl_s.at[0], dl_r.at[src], col=src).wait_recv()
        dl_sum = dl_sum + dl_in[src].astype(F32)
    dl_own[...] = dl_sum.astype(BF)
    dr_sum = dr_sib[chip].astype(F32)
    for d in range(1, n_chip):
        src = lax.rem(chip + n_chip - d, n_chip)
        remote(dr_in.at[src], dr_in.at[src], dr_s.at[d], dr_r.at[src], row=src * 2 + core).wait_recv()
        dr_sum = dr_sum + dr_in[src].astype(F32)
    dr_own[...] = dr_sum

    gain = jnp.zeros((1, M), F32)
    wgrad = jnp.zeros((2 * C, M), F32)
    for t in range(T):
        dcat = jnp.concatenate(
            [dl_own[t * C:(t + 1) * C, :], dr_own[pl.ds(t, C, stride=T), :].astype(BF)], axis=0)
        wgrad = wgrad + mm(dcat, nm[t])
        dn = mm_tn(dcat, wcat)
        xhat = xh[t]
        gain = gain + jnp.sum(dn * xhat, axis=0, keepdims=True)
        hid = dn * gamma
        m1 = jnp.mean(hid, axis=1, keepdims=True)
        m2 = jnp.mean(hid * xhat, axis=1, keepdims=True)
        rstd = rs[t]
        rstd = jnp.concatenate([rstd] * wide, axis=1)
        grad = rstd * (hid - m1 - xhat * m2)
        for a in range(wide):
            xs[a, pl.ds(t, S, stride=T), :] = grad[:, a * K:(a + 1) * K]
    grads = jnp.concatenate([xs[a] for a in range(wide)], axis=1)
    ag_buf[...] = grads.reshape(S, T, M).astype(BF)
    ag_copy = pltpu.make_async_copy(ag_buf, ag_hbm, ag_sem)
    ag_copy.start()

    RS = 2 * C
    for a in range(wide):
        sm_own[a, 0:RS, :] = wgrad[:, a * K:(a + 1) * K]
        sm_own[a, RS:RS + 16, :] = jnp.broadcast_to(gain[:, a * K:(a + 1) * K], (16, K))
    sm_to_sib = remote(sm_own.at[1 - core], sm_sib, s1_s, s1_r, row=sib)
    send(sm_to_sib)

    def sum_chips(own, got, ss, rr):
        total = own
        for d in range(1, n_chip):
            src = lax.rem(chip + n_chip - d, n_chip)
            remote(got.at[src], got.at[src], ss.at[d], rr.at[src], row=src * 2 + core).wait_recv()
            total = total + got[src].astype(F32)
        return total

    def sum_cols(own, got, ss, rr):
        total = own
        for d in range(1, n_col):
            src = lax.rem(col + n_col - d, n_col)
            remote(got.at[src], got.at[src], ss.at[d], rr.at[src], col=src).wait_recv()
            total = total + got[src].astype(F32)
        return total

    def to_chips(src, dst, ss, rr):
        for d in range(1, n_chip):
            peer = other_chip(d) * 2 + core
            send(remote(src, dst.at[chip], ss.at[d], rr.at[chip], row=peer))

    def to_cols(src, dst, ss, rr):
        for d in range(1, n_col):
            send(remote(src, dst.at[col], ss.at[d], rr.at[col], col=other_col(d)))

    def z_step(p):
        rhs = jnp.concatenate([
            jnp.concatenate([
                buf[(2 * p + a) * C:(2 * p + a + 1) * C, e * J:(e + 1) * J] for e in range(C)], axis=0)
            for a in range(2)], axis=1)
        res = mm(wpt[...], rhs) * inv
        for a in range(2):
            z_buf[(2 * p + a) * J:(2 * p + a + 1) * J, :] = res[:, a * J:(a + 1) * J].T.astype(BF)

    z_copies = []
    def z_part(n, of):
        lo, hi = n * (I // 2) // of, (n + 1) * (I // 2) // of
        for p in range(lo, hi):
            z_step(p)
        rows = pl.ds(lo * 2 * J, (hi - lo) * 2 * J)
        c = pltpu.make_async_copy(z_buf.at[rows], z_hbm.at[rows], z_sem.at[n])
        c.start()
        z_copies.append(c)

    def put_dw(h):
        per = RW // C
        for e in range(C // 2):
            part = dw_full[h, e // per].astype(F32)
            dwo_ref[pl.ds(h * (C // 2) + e, C, stride=C), :] = part[(e % per) * C:(e % per + 1) * C]

    z_part(0, 4)
    sm_to_sib.wait_recv()
    sm_give[...] = sm_own[core] + sm_sib[...]
    sm_out[0] = sm_give[...].astype(BF)
    to_cols(sm_out.at[0], sm_col, s2_s, s2_r)
    z_part(1, 4)
    own = dw_pair[col].astype(F32)
    dw_blk[0] = sum_cols(own, dw_in, d2_s, d2_r).astype(BF)
    to_chips(dw_blk.at[0], dw_chip, d3_s, d3_r)
    z_part(2, 4)
    sm_sum[...] = sum_cols(sm_give[...], sm_col, s2_s, s2_r)
    sm_out[1] = sm_sum[...].astype(BF)
    to_chips(sm_out.at[1], sm_chip, s3_s, s3_r)
    z_part(3, 4)
    dw_blk[1] = (sum_chips(dw_blk[0].astype(F32), dw_chip, d3_s, d3_r) * inv).astype(BF)
    to_cols(dw_blk.at[1], dw_full.at[core], d4_s, d4_r)
    dw_full[core, col] = dw_blk[1]
    sm_half[core] = sum_chips(sm_sum[...], sm_chip, s3_s, s3_r)
    sm_back = remote(sm_half.at[core], sm_half.at[core], s4_s, s4_r.at[core], row=sib)
    send(sm_back)
    for d in range(1, n_col):
        src = lax.rem(col + n_col - d, n_col)
        got = dw_full.at[core, src]
        remote(got, got, d4_s.at[d], d4_r.at[src], col=src).wait_recv()
    send(remote(dw_full.at[core], dw_full.at[core], d5_s, d5_r.at[core], row=sib))
    put_dw(core)

    got = sm_half.at[1 - core]
    remote(got, got, s4_s, s4_r.at[1 - core], row=sib).wait_recv()
    for a in range(wide):
        lanes = slice(a * K, (a + 1) * K)
        wl_ref[:, lanes] = sm_half[a, 0:C, :]
        wr_ref[:, lanes] = sm_half[a, C:2 * C, :]
        gain_ref[:, lanes] = sm_half[a, RS:RS + 1, :]
    got = dw_full.at[1 - core]
    remote(got, got, d5_s, d5_r.at[1 - core], row=sib).wait_recv()
    put_dw(1 - core)

    ag_copy.wait()
    for c in z_copies:
        c.wait()
    for c in pending:
        c.wait_send()


def settle_kernel(*refs):
    n = (len(refs) - 2) // 3
    srcs, dsts, held = refs[:n], refs[n:2 * n], refs[2 * n:3 * n]
    in_sems, out_sems = refs[3 * n:]
    loads, stores = [], []
    for src, dst, mid in zip(srcs, dsts, held):
        parts = 4 if src.shape[0] >= 4096 else 1
        rows = src.shape[0] // parts
        for p in range(parts):
            part = pl.ds(p * rows, rows)
            k = len(loads)
            loads.append(pltpu.make_async_copy(src.at[part], mid.at[part], in_sems.at[k]))
            stores.append(pltpu.make_async_copy(mid.at[part], dst.at[part], out_sems.at[k]))
            loads[-1].start()
    for load, store in zip(loads, stores):
        load.wait()
        store.start()
    for store in stores:
        store.wait()


def settle(arrays):
    hb = pl.BlockSpec(memory_space=pl.ANY)
    sems = pltpu.SemaphoreType.DMA((len(arrays) + 3,))
    return pl.pallas_call(
        settle_kernel,
        out_shape=tuple(jax.ShapeDtypeStruct(a.shape, a.dtype) for a in arrays),
        in_specs=[hb] * len(arrays),
        out_specs=(hb,) * len(arrays),
        scratch_shapes=[pltpu.VMEM(a.shape, a.dtype) for a in arrays] + [sems, sems],
        compiler_params=pltpu.CompilerParams(vmem_limit_bytes=62 * 1024 * 1024),
    )(*arrays)


def on_device(n_row, n_col, x, gamma, w1, w2, wo, cot):
    S, T, M = x.shape
    C = w1.shape[1]
    CC, K = wo.shape
    I, J = cot.shape[0], cot.shape[1] * cot.shape[2]
    B = T * C
    n_chip = n_row // 2
    RW = CC // 2 // n_col
    RS = 2 * C + 16
    one = pltpu.SemaphoreType.DMA
    V = lambda shape, dtype: pltpu.VMEM(shape, dtype)
    D = lambda n: pltpu.SemaphoreType.DMA((n,))
    vm = pl.BlockSpec(memory_space=pltpu.VMEM)
    hb = pl.BlockSpec(memory_space=pl.ANY)
    z, ag, wl, wr, dwo, gain = pl.pallas_call(
        functools.partial(kernel, n_row, n_col),
        out_shape=(
            jax.ShapeDtypeStruct((I * J, K), BF),
            jax.ShapeDtypeStruct((S, T, M), BF),
            jax.ShapeDtypeStruct((C, M), F32),
            jax.ShapeDtypeStruct((C, M), F32),
            jax.ShapeDtypeStruct((CC, K), F32),
            jax.ShapeDtypeStruct((1, M), F32),
        ),
        in_specs=[vm, vm, vm, vm, vm, hb],
        out_specs=(hb, hb, vm, vm, vm, vm),
        scratch_shapes=[
            V((I * J, K), BF),
            V((M // K, S * T, K), F32),
            V((T, S, M), F32),
            V((T, S, M), BF),
            V((T, S, K), F32),
            V((CC, K), BF),
            V((K, CC), BF),
            V((CC, K), F32),
            V((B, S), F32),
            V((n_row, B, S), BF),
            V((C * J, S), BF),
            V((I * C, S), BF),
            V((2, S, I * C // 2), BF),
            V((CC, I * J), BF),
            V((I * C, C * J), BF),
            V((n_col, B, S), BF),
            V((n_col, B, S), BF),
            V((S, C * J), F32),
            V((2, n_chip, B, S), BF),
            V((n_chip, B, S), BF),
            V((n_chip, B, S), BF),
            V((B, S), BF),
            V((B, S), F32),
            V((CC // 2, K), BF),
            V((CC // 2, K), BF),
            V((CC // 2, K), F32),
            V((n_col, RW, K), BF),
            V((n_col, RW, K), BF),
            V((2, RW, K), BF),
            V((n_chip, RW, K), BF),
            V((2, n_col, RW, K), BF),
            V((RS, K), F32),
            V((RS, K), F32),
            V((2, RS, K), F32),
            V((2, RS, K), BF),
            V((n_col, RS, K), BF),
            V((RS, K), F32),
            V((n_chip, RS, K), BF),
            V((2, RS, K), F32),
            V((I * J, K), BF),
            V((S, T, M), BF),
            one, D(4), one,
            D(n_row), D(n_row), D(n_col), D(n_col), D(n_col), D(n_col), D(n_chip), D(n_chip + 1),
            one, one, D(n_col), D(n_col), D(n_chip), D(n_chip), D(n_col), D(n_col), one, D(2),
            one, one, D(n_col), D(n_col), D(n_chip), D(n_chip), one, D(2),
        ],
        compiler_params=pltpu.CompilerParams(
            collective_id=0, has_side_effects=True, vmem_limit_bytes=56 * 1024 * 1024,
        ),
    )(x, gamma.reshape(1, M), w1.T, w2.T, wo, cot.reshape(I * J, K))
    z, ag, wl, wr, dwo, gain = settle((z, ag, wl, wr, dwo, gain))
    return z.reshape(cot.shape), ag, wl.T, wr.T, dwo, gain.reshape(M)


def solution(mesh):
    placed = (P(None, ("row", "col"), None), P(), P(), P(), P(), P("row", None, "col", None))
    return jax.shard_map(
        functools.partial(on_device, mesh.shape["row"], mesh.shape["col"]),
        mesh=mesh,
        in_specs=placed,
        out_specs=(P("row", None, "col", None), P(None, ("row", "col"), None), P(), P(), P(), P()),
        check_vma=False,
    )
```

```python
import functools

import jax
import jax.numpy as jnp
from jax import lax
from jax.experimental import pallas as pl
from jax.experimental.pallas import tpu as pltpu
from jax.sharding import PartitionSpec as P

MESH = pl.DeviceIdType.MESH
BF = jnp.bfloat16
F32 = jnp.float32
NT = (((1,), (1,)), ((), ()))
TN = (((0,), (0,)), ((), ()))


def mm(a, b):
    return jnp.dot(a, b, preferred_element_type=F32)


def mm_nt(a, b):
    return lax.dot_general(a, b, NT, preferred_element_type=F32)


def mm_tn(a, b):
    return lax.dot_general(a, b, TN, preferred_element_type=F32)


def remote(src, dst, send_sem, recv_sem, **where):
    return pltpu.make_async_remote_copy(
        src_ref=src, dst_ref=dst, send_sem=send_sem, recv_sem=recv_sem,
        device_id=where, device_id_type=MESH,
    )


def aligned(start, size, multiple):
    return pl.ds(pl.multiple_of(start, multiple), size)


def kernel(
    n_row, n_col,
    x_hbm, gamma_hbm, w1_hbm, w2_hbm, wo_hbm, g_hbm,
    z_hbm, ag_hbm, wl_hbm, wr_hbm, dwo_hbm, gain_hbm,
    x_ref, gamma_ref, w1_ref, w2_ref, wo_ref,
    g_ref, xs, xh, nm, rs, wp, wpt, wf, rf, right_in, right, left, left_t, g_out, buf,
    dl_out, dl_in, dr_acc, dr_out, dr_sib, dr_in, dl_own, dr_own,
    dw_give, dw_sib, dw_own, dw_pair, dw_in, dw_blk, dw_chip, dw_full,
    sm_give, sm_sib, sm_own, sm_out, sm_col, sm_sum, sm_chip, sm_half, z_buf, ag_buf, wl, wr, dwo, gain_buf,
    in_sem, g_sem, z_sem, ag_sem, out_sem, rg_s, rg_r, lg_s, lg_r, dl_s, dl_r, dr_s, dr_r,
    d1_s, d1_r, d2_s, d2_r, d3_s, d3_r, d4_s, d4_r,
    s1_s, s1_r, s2_s, s2_r, s3_s, s3_r, s4_s, s4_r,
):
    S, T, M = x_ref.shape
    C = w1_ref.shape[0]
    CC, K = wo_ref.shape
    J = n_row * T
    I = n_col * T
    B = T * C
    n_chip = n_row // 2
    inv = 1.0 / S
    row = lax.axis_index("row")
    col = lax.axis_index("col")
    chip = row // 2
    core = lax.rem(row, 2)
    sib = chip * 2 + 1 - core
    n_x, n_y = n_row // 4, n_col // 2
    x, zh = row // 4, lax.rem(row, 4) // 2
    zl, y = col // n_y, lax.rem(col, n_y)

    def row_of(dx, far, other):
        z = 1 - zh if far else zh
        return lax.rem(x + dx, n_x) * 4 + z * 2 + (1 - core if other else core)

    def col_of(dy, far):
        return (1 - zl if far else zl) * n_y + lax.rem(y + dy, n_y)

    pending = []

    def send(c):
        c.start()
        pending.append(c)

    def other_col(d):
        return lax.rem(col + d, n_col)

    def other_chip(d):
        return lax.rem(chip + d, n_chip)

    barrier = pltpu.get_barrier_semaphore()
    pl.semaphore_signal(barrier, inc=1, device_id={"row": sib}, device_id_type=MESH)
    for d in range(1, n_chip):
        peer = other_chip(d) * 2 + core
        pl.semaphore_signal(barrier, inc=1, device_id={"row": peer}, device_id_type=MESH)
    for d in range(1, n_col):
        pl.semaphore_signal(barrier, inc=1, device_id={"col": other_col(d)}, device_id_type=MESH)
        pl.semaphore_signal(
            barrier, inc=1, device_id={"row": sib, "col": other_col(d)}, device_id_type=MESH)

    loads = [
        pltpu.make_async_copy(src, dst, in_sem.at[k])
        for k, (src, dst) in enumerate((
            (x_hbm, x_ref), (gamma_hbm, gamma_ref), (w1_hbm, w1_ref), (w2_hbm, w2_ref), (wo_hbm, wo_ref)))
    ]
    for c in loads:
        c.start()
    g_copy = pltpu.make_async_copy(g_hbm, g_ref, g_sem)
    g_copy.start()
    for c in loads[:4]:
        c.wait()

    wcat = jnp.concatenate([w1_ref[...], w2_ref[...]], axis=0)
    gamma = gamma_ref[...]
    wide = M // K
    x_all = x_ref[...].astype(F32).reshape(S * T, M)
    for a in range(wide):
        xs[a] = x_all[:, a * K:(a + 1) * K]
    for t in range(T):
        xt = jnp.concatenate([xs[a, pl.ds(t, S, stride=T), :] for a in range(wide)], axis=1)
        center = xt - jnp.mean(xt, axis=1, keepdims=True)
        rstd = lax.rsqrt(jnp.mean(center * center, axis=1, keepdims=True) + 1e-05)
        xhat = center * rstd
        normed = (xhat * gamma).astype(BF)
        xh[t] = xhat
        nm[t] = normed
        rs[t] = jnp.broadcast_to(rstd, (S, K))
        proj = mm_nt(wcat, normed)
        left[aligned(col * B + t * C, C, C), :] = proj[:C].astype(BF)
        rf[pl.ds(t, C, stride=T), :] = proj[C:]
    right_in[row] = rf[...].astype(BF)

    pl.semaphore_wait(barrier, n_chip + 2 * (n_col - 1))

    def left_rows(c):
        return aligned(c * B, B, B)

    def send_right(block, slot, to):
        send(remote(right_in.at[block], right_in.at[block], rg_s.at[slot], rg_r.at[block], row=to))

    def wait_right(block):
        remote(right_in.at[block], right_in.at[block], rg_s.at[0], rg_r.at[block], row=sib).wait_recv()

    def send_left(block, slot, to):
        rows = left_rows(block)
        send(remote(left.at[rows], left.at[rows], lg_s.at[slot], lg_r.at[block], col=to))

    def wait_left(block):
        rows = left_rows(block)
        remote(left.at[rows], left.at[rows], lg_s.at[0], lg_r.at[block], col=col_of(0, True)).wait_recv()

    send_right(row, 0, row_of(0, True, False))
    send_left(col, 0, col_of(0, True))
    for d in range(1, n_x):
        send_right(row, d, row_of(d, False, False))
    for d in range(1, n_y):
        send_left(col, d, col_of(d, False))
    send_right(row, 2 * n_x, sib)

    loads[4].wait()
    wf[...] = wo_ref[...].astype(F32)
    for e in range(C):
        wp[e * C:(e + 1) * C, :] = wf[pl.ds(e, C, stride=C), :].astype(BF)
    wpt[...] = wp[...].astype(F32).T.astype(BF)

    g_copy.wait()
    GN = 4 * J

    def g_outer_part(lo, hi):
        for n in range(lo, hi):
            cols = slice(n * GN, (n + 1) * GN)
            g_out[:, cols] = mm_nt(wp[...], g_ref[cols, :]).astype(BF)

    n_go = I * J // GN
    g_outer_part(0, n_go // 2)

    far_row, far_col = row_of(0, True, False), col_of(0, True)
    wait_right(far_row)
    for d in range(1, n_x):
        send_right(far_row, n_x + d, row_of(d, False, False))
    send_right(far_row, n_x, sib)
    wait_left(far_col)
    for d in range(1, n_y):
        send_left(far_col, n_y + d, col_of(d, False))

    g_outer_part(n_go // 2, n_go)

    HB = n_col // 2 * B
    HI = I // 2

    def turn_left(z, h):
        for k in range(HB // S):
            left_t[h, :, k * S:(k + 1) * S] = left[aligned(z * HB + k * S, S, S), :].T

    def right_grad(z, h, p):
        rhs = jnp.concatenate([
            jnp.concatenate([
                g_out[(2 * p + a) * C:(2 * p + a + 1) * C, aligned((z * HI + i) * J, J, J)]
                for a in range(2)], axis=1)
            for i in range(HI)], axis=0)
        return mm(left_t[h], rhs)

    for d in range(1, n_y):
        wait_left(col_of(d, False))
    turn_left(zl, 0)
    for p in range(C // 2):
        dr_acc[:, 2 * p * J:(2 * p + 2) * J] = right_grad(zl, 0, p)

    for d in range(1, n_x):
        block = row_of(d, False, False)
        wait_right(block)
        send_right(block, 2 * n_x + d, sib)
    for d in range(1, n_y):
        wait_left(col_of(d, True))
    turn_left(1 - zl, 1)
    for p in range(C // 2):
        if p == C // 8:
            for d in range(1, n_x):
                block = row_of(d, True, False)
                wait_right(block)
                send_right(block, 3 * n_x + d, sib)
        acc = (dr_acc[:, 2 * p * J:(2 * p + 2) * J] + right_grad(1 - zl, 1, p)) * inv
        tiles = [acc[:, a * J:(a + 1) * J].T for a in range(2)]
        for q in range(n_row):
            blk = jnp.concatenate([t[q * T:(q + 1) * T] for t in tiles], axis=0)
            dr_out[q % 2, q // 2, p * 2 * T:(p + 1) * 2 * T, :] = blk.astype(BF)
    to_sib = remote(dr_out.at[1 - core], dr_sib, dr_s.at[0], dr_r.at[n_chip], row=sib)
    send(to_sib)

    for far in (False, True):
        for d in range(n_x):
            wait_right(row_of(d, far, True))
    def right_step(h, _):
        parts = [right_in[q, aligned(h * 2 * T, 2 * T, 2 * T), :].astype(F32) for q in range(n_row)]
        for a in range(2):
            tile = jnp.concatenate([p[a * T:(a + 1) * T] for p in parts], axis=0)
            right[aligned((2 * h + a) * J, J, J), :] = tile.astype(BF)
        return 0
    lax.fori_loop(0, C // 2, right_step, 0)

    def right_grad_out():
        to_sib.wait_recv()
        def pair_step(q, _):
            dr_sib[q] = (dr_out[core, q].astype(F32) + dr_sib[q].astype(F32)).astype(BF)
            return 0
        lax.fori_loop(0, n_chip, pair_step, 0)
        for d in range(1, n_chip):
            peer = other_chip(d)
            send(remote(dr_sib.at[peer], dr_in.at[chip], dr_s.at[d], dr_r.at[chip], row=peer * 2 + core))

    for k in range(n_col):
        owner = other_col(k + 1) if k < n_col - 1 else col
        lhs = jnp.concatenate([
            jnp.concatenate([
                g_out[e * C:(e + 1) * C, aligned((owner * T + t) * J, J, J)] for t in range(T)], axis=0)
            for e in range(C)], axis=1)
        dl_out[owner] = (mm(lhs, right[...]) * inv).astype(BF)
        if k == n_col // 2 - 1:
            right_grad_out()
        if k < n_col - 1:
            send(remote(dl_out.at[owner], dl_in.at[col], dl_s.at[k], dl_r.at[col], col=owner))

    RB = I * C // 2
    NB = 4 * J
    for k in range(2):
        for n in range(C * J // NB):
            res = mm_nt(left[k * RB:(k + 1) * RB, :], right[n * NB:(n + 1) * NB, :])
            buf[k * RB:(k + 1) * RB, n * NB:(n + 1) * NB] = res.astype(BF)

    HW = CC // 2
    QE = C // 4

    def dw_quarter(e0):
        lhs = jnp.concatenate([
            jnp.concatenate([
                buf[i * C:(i + 1) * C, aligned((e0 + e) * J, J, J)] for e in range(QE)], axis=0)
            for i in range(I)], axis=1)
        return mm(lhs, g_ref[...])

    for q in range(2):
        rows = slice(q * HW // 2, (q + 1) * HW // 2)
        dw_give[rows, :] = dw_quarter((1 - core) * 2 * QE + q * QE).astype(BF)
    dw_to_sib = remote(dw_give, dw_sib, d1_s, d1_r, row=sib)
    send(dw_to_sib)
    for q in range(2):
        rows = slice(q * HW // 2, (q + 1) * HW // 2)
        dw_own[rows, :] = dw_quarter(core * 2 * QE + q * QE)

    RW = HW // n_col
    dw_to_sib.wait_recv()
    dw_pair[...] = (dw_own[...] + dw_sib[...].astype(F32)).astype(BF).reshape(n_col, RW, K)
    for d in range(1, n_col):
        peer = other_col(d)
        send(remote(dw_pair.at[peer], dw_in.at[col], d2_s.at[d], d2_r.at[col], col=peer))

    dl_sum = dl_out[col].astype(F32)
    for d in range(1, n_col):
        src = lax.rem(col + n_col - d, n_col)
        remote(dl_in.at[src], dl_in.at[src], dl_s.at[0], dl_r.at[src], col=src).wait_recv()
        dl_sum = dl_sum + dl_in[src].astype(F32)
    dl_own[...] = dl_sum.astype(BF)
    dr_sum = dr_sib[chip].astype(F32)
    for d in range(1, n_chip):
        src = lax.rem(chip + n_chip - d, n_chip)
        remote(dr_in.at[src], dr_in.at[src], dr_s.at[d], dr_r.at[src], row=src * 2 + core).wait_recv()
        dr_sum = dr_sum + dr_in[src].astype(F32)
    dr_own[...] = dr_sum

    gain = jnp.zeros((1, M), F32)
    wgrad = jnp.zeros((2 * C, M), F32)
    for t in range(T):
        dcat = jnp.concatenate(
            [dl_own[t * C:(t + 1) * C, :], dr_own[pl.ds(t, C, stride=T), :].astype(BF)], axis=0)
        wgrad = wgrad + mm(dcat, nm[t])
        dn = mm_tn(dcat, wcat)
        xhat = xh[t]
        gain = gain + jnp.sum(dn * xhat, axis=0, keepdims=True)
        hid = dn * gamma
        m1 = jnp.mean(hid, axis=1, keepdims=True)
        m2 = jnp.mean(hid * xhat, axis=1, keepdims=True)
        rstd = rs[t]
        rstd = jnp.concatenate([rstd] * wide, axis=1)
        grad = rstd * (hid - m1 - xhat * m2)
        for a in range(wide):
            xs[a, pl.ds(t, S, stride=T), :] = grad[:, a * K:(a + 1) * K]
    grads = jnp.concatenate([xs[a] for a in range(wide)], axis=1)
    ag_buf[...] = grads.reshape(S, T, M).astype(BF)
    ag_copy = pltpu.make_async_copy(ag_buf, ag_hbm, ag_sem)
    ag_copy.start()

    RS = 2 * C
    for a in range(wide):
        sm_own[a, 0:RS, :] = wgrad[:, a * K:(a + 1) * K]
        sm_own[a, RS:RS + 16, :] = jnp.broadcast_to(gain[:, a * K:(a + 1) * K], (16, K))
    sm_to_sib = remote(sm_own.at[1 - core], sm_sib, s1_s, s1_r, row=sib)
    send(sm_to_sib)

    def sum_chips(own, got, ss, rr):
        total = own
        for d in range(1, n_chip):
            src = lax.rem(chip + n_chip - d, n_chip)
            remote(got.at[src], got.at[src], ss.at[d], rr.at[src], row=src * 2 + core).wait_recv()
            total = total + got[src].astype(F32)
        return total

    def sum_cols(own, got, ss, rr):
        total = own
        for d in range(1, n_col):
            src = lax.rem(col + n_col - d, n_col)
            remote(got.at[src], got.at[src], ss.at[d], rr.at[src], col=src).wait_recv()
            total = total + got[src].astype(F32)
        return total

    def to_chips(src, dst, ss, rr):
        for d in range(1, n_chip):
            peer = other_chip(d) * 2 + core
            send(remote(src, dst.at[chip], ss.at[d], rr.at[chip], row=peer))

    def to_cols(src, dst, ss, rr):
        for d in range(1, n_col):
            send(remote(src, dst.at[col], ss.at[d], rr.at[col], col=other_col(d)))

    def z_step(p):
        rhs = jnp.concatenate([
            jnp.concatenate([
                buf[(2 * p + a) * C:(2 * p + a + 1) * C, e * J:(e + 1) * J] for e in range(C)], axis=0)
            for a in range(2)], axis=1)
        res = mm(wpt[...], rhs) * inv
        for a in range(2):
            z_buf[(2 * p + a) * J:(2 * p + a + 1) * J, :] = res[:, a * J:(a + 1) * J].T.astype(BF)

    z_copies = []
    def z_part(n, of):
        lo, hi = n * (I // 2) // of, (n + 1) * (I // 2) // of
        for p in range(lo, hi):
            z_step(p)
        rows = pl.ds(lo * 2 * J, (hi - lo) * 2 * J)
        c = pltpu.make_async_copy(z_buf.at[rows], z_hbm.at[rows], z_sem.at[n])
        c.start()
        z_copies.append(c)

    z_part(0, 4)
    sm_to_sib.wait_recv()
    sm_give[...] = sm_own[core] + sm_sib[...]
    sm_out[0] = sm_give[...].astype(BF)
    to_cols(sm_out.at[0], sm_col, s2_s, s2_r)
    z_part(1, 4)
    own = dw_pair[col].astype(F32)
    dw_blk[0] = sum_cols(own, dw_in, d2_s, d2_r).astype(BF)
    to_chips(dw_blk.at[0], dw_chip, d3_s, d3_r)
    z_part(2, 4)
    sm_sum[...] = sum_cols(sm_give[...], sm_col, s2_s, s2_r)
    sm_out[1] = sm_sum[...].astype(BF)
    to_chips(sm_out.at[1], sm_chip, s3_s, s3_r)
    z_part(3, 4)
    dw_blk[1] = (sum_chips(dw_blk[0].astype(F32), dw_chip, d3_s, d3_r) * inv).astype(BF)
    def give_dw(slot, **where):
        send(remote(dw_blk.at[1], dw_full.at[core, col], d4_s.at[slot], d4_r.at[core, col], **where))

    for d in range(1, n_col):
        give_dw(d, col=other_col(d))
        give_dw(n_col + d, row=sib, col=other_col(d))
    give_dw(0, row=sib)
    dw_full[core, col] = dw_blk[1]
    sm_half[core] = sum_chips(sm_sum[...], sm_chip, s3_s, s3_r)
    sm_back = remote(sm_half.at[core], sm_half.at[core], s4_s, s4_r.at[core], row=sib)
    send(sm_back)
    def wait_dw(h, src):
        got = dw_full.at[h, src]
        remote(got, got, d4_s.at[0], d4_r.at[h, src], row=sib).wait_recv()

    for d in range(1, n_col):
        wait_dw(core, lax.rem(col + n_col - d, n_col))

    def put_dw(h):
        per = RW // C
        for e in range(C // 2):
            part = dw_full[h, e // per, (e % per) * C:(e % per + 1) * C, :]
            dwo[pl.ds(h * (C // 2) + e, C, stride=C), :] = part.astype(F32)

    put_dw(core)

    got = sm_half.at[1 - core]
    remote(got, got, s4_s, s4_r.at[1 - core], row=sib).wait_recv()
    for a in range(wide):
        lanes = slice(a * K, (a + 1) * K)
        wl[:, lanes] = sm_half[a, 0:C, :]
        wr[:, lanes] = sm_half[a, C:2 * C, :]
        gain_buf[:, lanes] = sm_half[a, RS:RS + 1, :]
    outs = []

    def put(src, dst):
        outs.append(pltpu.make_async_copy(src, dst, out_sem.at[len(outs)]))
        outs[-1].start()

    put(wl, wl_hbm)
    put(wr, wr_hbm)
    put(gain_buf, gain_hbm)
    for d in range(n_col):
        wait_dw(1 - core, lax.rem(col + n_col - d, n_col))
    put_dw(1 - core)
    put(dwo, dwo_hbm)
    for c in outs:
        c.wait()

    ag_copy.wait()
    for c in z_copies:
        c.wait()
    for c in pending:
        c.wait_send()


def settle_kernel(*refs):
    n = (len(refs) - 2) // 3
    srcs, dsts, held = refs[:n], refs[n:2 * n], refs[2 * n:3 * n]
    in_sems, out_sems = refs[3 * n:]
    loads, stores = [], []
    for src, dst, mid in zip(srcs, dsts, held):
        parts = 4 if src.shape[0] >= 4096 else 1
        rows = src.shape[0] // parts
        for p in range(parts):
            part = pl.ds(p * rows, rows)
            k = len(loads)
            loads.append(pltpu.make_async_copy(src.at[part], mid.at[part], in_sems.at[k]))
            stores.append(pltpu.make_async_copy(mid.at[part], dst.at[part], out_sems.at[k]))
            loads[-1].start()
    for load, store in zip(loads, stores):
        load.wait()
        store.start()
    for store in stores:
        store.wait()


def settle(arrays):
    hb = pl.BlockSpec(memory_space=pl.ANY)
    sems = pltpu.SemaphoreType.DMA((len(arrays) + 3,))
    return pl.pallas_call(
        settle_kernel,
        out_shape=tuple(jax.ShapeDtypeStruct(a.shape, a.dtype) for a in arrays),
        in_specs=[hb] * len(arrays),
        out_specs=(hb,) * len(arrays),
        scratch_shapes=[pltpu.VMEM(a.shape, a.dtype) for a in arrays] + [sems, sems],
        compiler_params=pltpu.CompilerParams(vmem_limit_bytes=62 * 1024 * 1024),
    )(*arrays)


def on_device(n_row, n_col, x, gamma, w1, w2, wo, cot):
    S, T, M = x.shape
    C = w1.shape[1]
    CC, K = wo.shape
    I, J = cot.shape[0], cot.shape[1] * cot.shape[2]
    B = T * C
    n_chip = n_row // 2
    RW = CC // 2 // n_col
    RS = 2 * C + 16
    one = pltpu.SemaphoreType.DMA
    V = lambda shape, dtype: pltpu.VMEM(shape, dtype)
    D = lambda n: pltpu.SemaphoreType.DMA((n,))
    hb = pl.BlockSpec(memory_space=pl.ANY)
    parts = pl.pallas_call(
        functools.partial(kernel, n_row, n_col),
        out_shape=(
            jax.ShapeDtypeStruct((I * J, K), BF),
            jax.ShapeDtypeStruct((S, T, M), BF),
            jax.ShapeDtypeStruct((C, M), F32),
            jax.ShapeDtypeStruct((C, M), F32),
            jax.ShapeDtypeStruct((CC, K), F32),
            jax.ShapeDtypeStruct((1, M), F32),
        ),
        in_specs=[hb] * 6,
        out_specs=(hb,) * 6,
        scratch_shapes=[
            V((S, T, M), BF),
            V((1, M), F32),
            V((C, M), BF),
            V((C, M), BF),
            V((CC, K), BF),
            V((I * J, K), BF),
            V((M // K, S * T, K), F32),
            V((T, S, M), F32),
            V((T, S, M), BF),
            V((T, S, K), F32),
            V((CC, K), BF),
            V((K, CC), BF),
            V((CC, K), F32),
            V((B, S), F32),
            V((n_row, B, S), BF),
            V((C * J, S), BF),
            V((I * C, S), BF),
            V((2, S, I * C // 2), BF),
            V((CC, I * J), BF),
            V((I * C, C * J), BF),
            V((n_col, B, S), BF),
            V((n_col, B, S), BF),
            V((S, C * J), F32),
            V((2, n_chip, B, S), BF),
            V((n_chip, B, S), BF),
            V((n_chip, B, S), BF),
            V((B, S), BF),
            V((B, S), F32),
            V((CC // 2, K), BF),
            V((CC // 2, K), BF),
            V((CC // 2, K), F32),
            V((n_col, RW, K), BF),
            V((n_col, RW, K), BF),
            V((2, RW, K), BF),
            V((n_chip, RW, K), BF),
            V((2, n_col, RW, K), BF),
            V((RS, K), F32),
            V((RS, K), F32),
            V((2, RS, K), F32),
            V((2, RS, K), BF),
            V((n_col, RS, K), BF),
            V((RS, K), F32),
            V((n_chip, RS, K), BF),
            V((2, RS, K), F32),
            V((I * J, K), BF),
            V((S, T, M), BF),
            V((C, M), F32),
            V((C, M), F32),
            V((CC, K), F32),
            V((1, M), F32),
            D(5), one, D(4), one, D(4),
            D(n_row), D(n_row), D(n_col), D(n_col), D(n_col), D(n_col), D(n_chip), D(n_chip + 1),
            one, one, D(n_col), D(n_col), D(n_chip), D(n_chip), D(2 * n_col), pltpu.SemaphoreType.DMA((2, n_col)),
            one, one, D(n_col), D(n_col), D(n_chip), D(n_chip), one, D(2),
        ],
        compiler_params=pltpu.CompilerParams(
            collective_id=0, has_side_effects=True, vmem_limit_bytes=56 * 1024 * 1024,
        ),
    )(x, gamma.reshape(1, M), w1.T, w2.T, wo, cot.reshape(I * J, K))
    z, ag, wl, wr, dwo, gain = settle(parts)
    return z.reshape(cot.shape), ag, wl.T, wr.T, dwo, gain.reshape(M)


def solution(mesh):
    placed = (P(None, ("row", "col"), None), P(), P(), P(), P(), P("row", None, "col", None))
    return jax.shard_map(
        functools.partial(on_device, mesh.shape["row"], mesh.shape["col"]),
        mesh=mesh,
        in_specs=placed,
        out_specs=(P("row", None, "col", None), P(None, ("row", "col"), None), P(), P(), P(), P()),
        check_vma=False,
    )
```

```python
import functools

import jax
import jax.numpy as jnp
from jax import lax
from jax.experimental import pallas as pl
from jax.experimental.pallas import tpu as pltpu
from jax.sharding import PartitionSpec as P

MESH = pl.DeviceIdType.MESH
BF = jnp.bfloat16
F32 = jnp.float32
NT = (((1,), (1,)), ((), ()))
TN = (((0,), (0,)), ((), ()))


def mm(a, b):
    return jnp.dot(a, b, preferred_element_type=F32)


def mm_nt(a, b):
    return lax.dot_general(a, b, NT, preferred_element_type=F32)


def mm_tn(a, b):
    return lax.dot_general(a, b, TN, preferred_element_type=F32)


def remote(src, dst, send_sem, recv_sem, **where):
    return pltpu.make_async_remote_copy(
        src_ref=src, dst_ref=dst, send_sem=send_sem, recv_sem=recv_sem,
        device_id=where, device_id_type=MESH,
    )


def aligned(start, size, multiple):
    return pl.ds(pl.multiple_of(start, multiple), size)


def kernel(
    n_row, n_col,
    x_hbm, gamma_hbm, w1_hbm, w2_hbm, wo_hbm, g_hbm,
    z_hbm, ag_hbm, wl_hbm, wr_hbm, dwo_hbm, gain_hbm,
    x_ref, gamma_ref, w1_ref, w2_ref, wo_ref,
    g_ref, xs, xh, nm, rs, wp, wpt, wf, rf, right_in, right, left, left_t, g_out, buf,
    dl_out, dl_in, dr_acc, dr_out, dr_sib, dr_in, dl_own, dr_own,
    dw_give, dw_sib, dw_own, dw_pair, dw_in, dw_blk, dw_chip, dw_full,
    sm_give, sm_sib, sm_own, sm_out, sm_col, sm_sum, sm_chip, sm_half, z_buf, ag_buf, wl, wr, dwo, gain_buf,
    in_sem, g_sem, z_sem, ag_sem, out_sem, rg_s, rg_r, lg_s, lg_r, dl_s, dl_r, dr_s, dr_r,
    d1_s, d1_r, d2_s, d2_r, d3_s, d3_r, d4_s, d4_r,
    s1_s, s1_r, s2_s, s2_r, s3_s, s3_r, s4_s, s4_r,
):
    S, T, M = x_ref.shape
    C = w1_ref.shape[0]
    CC, K = wo_ref.shape
    J = n_row * T
    I = n_col * T
    B = T * C
    n_chip = n_row // 2
    inv = 1.0 / S
    row = lax.axis_index("row")
    col = lax.axis_index("col")
    chip = row // 2
    core = lax.rem(row, 2)
    sib = chip * 2 + 1 - core
    n_x, n_y = n_row // 4, n_col // 2
    x, zh = row // 4, lax.rem(row, 4) // 2
    zl, y = col // n_y, lax.rem(col, n_y)

    def row_of(dx, far, other):
        z = 1 - zh if far else zh
        return lax.rem(x + dx, n_x) * 4 + z * 2 + (1 - core if other else core)

    def col_of(dy, far):
        return (1 - zl if far else zl) * n_y + lax.rem(y + dy, n_y)

    pending = []

    def send(c):
        c.start()
        pending.append(c)

    def other_col(d):
        return lax.rem(col + d, n_col)

    def other_chip(d):
        return lax.rem(chip + d, n_chip)

    barrier = pltpu.get_barrier_semaphore()
    pl.semaphore_signal(barrier, inc=1, device_id={"row": sib}, device_id_type=MESH)
    for d in range(1, n_chip):
        peer = other_chip(d) * 2 + core
        pl.semaphore_signal(barrier, inc=1, device_id={"row": peer}, device_id_type=MESH)
    for d in range(1, n_col):
        pl.semaphore_signal(barrier, inc=1, device_id={"col": other_col(d)}, device_id_type=MESH)
        pl.semaphore_signal(
            barrier, inc=1, device_id={"row": sib, "col": other_col(d)}, device_id_type=MESH)

    loads = [
        pltpu.make_async_copy(src, dst, in_sem.at[k])
        for k, (src, dst) in enumerate((
            (x_hbm, x_ref), (gamma_hbm, gamma_ref), (w1_hbm, w1_ref), (w2_hbm, w2_ref), (wo_hbm, wo_ref)))
    ]
    for c in loads:
        c.start()
    g_copy = pltpu.make_async_copy(g_hbm, g_ref, g_sem)
    g_copy.start()
    for c in loads[:4]:
        c.wait()

    wcat = jnp.concatenate([w1_ref[...], w2_ref[...]], axis=0)
    gamma = gamma_ref[...]
    wide = M // K
    x_all = x_ref[...].astype(F32).reshape(S * T, M)
    for a in range(wide):
        xs[a] = x_all[:, a * K:(a + 1) * K]
    for t in range(T):
        xt = jnp.concatenate([xs[a, pl.ds(t, S, stride=T), :] for a in range(wide)], axis=1)
        center = xt - jnp.mean(xt, axis=1, keepdims=True)
        rstd = lax.rsqrt(jnp.mean(center * center, axis=1, keepdims=True) + 1e-05)
        xhat = center * rstd
        normed = (xhat * gamma).astype(BF)
        xh[t] = xhat
        nm[t] = normed
        rs[t] = jnp.broadcast_to(rstd, (S, K))
        proj = mm_nt(wcat, normed)
        left[aligned(col * B + t * C, C, C), :] = proj[:C].astype(BF)
        rf[pl.ds(t, C, stride=T), :] = proj[C:]
    right_in[row] = rf[...].astype(BF)

    pl.semaphore_wait(barrier, n_chip + 2 * (n_col - 1))

    def left_rows(c):
        return aligned(c * B, B, B)

    def send_right(block, slot, to):
        send(remote(right_in.at[block], right_in.at[block], rg_s.at[slot], rg_r.at[block], row=to))

    def wait_right(block):
        remote(right_in.at[block], right_in.at[block], rg_s.at[0], rg_r.at[block], row=sib).wait_recv()

    def send_left(block, slot, to):
        rows = left_rows(block)
        send(remote(left.at[rows], left.at[rows], lg_s.at[slot], lg_r.at[block], col=to))

    def wait_left(block):
        rows = left_rows(block)
        remote(left.at[rows], left.at[rows], lg_s.at[0], lg_r.at[block], col=col_of(0, True)).wait_recv()

    send_right(row, 0, row_of(0, True, False))
    send_left(col, 0, col_of(0, True))
    for d in range(1, n_x):
        send_right(row, d, row_of(d, False, False))
    for d in range(1, n_y):
        send_left(col, d, col_of(d, False))
    send_right(row, 2 * n_x, sib)

    loads[4].wait()
    wf[...] = wo_ref[...].astype(F32)
    for e in range(C):
        wp[e * C:(e + 1) * C, :] = wf[pl.ds(e, C, stride=C), :].astype(BF)
    wpt[...] = wp[...].astype(F32).T.astype(BF)

    g_copy.wait()
    GN = 4 * J

    def g_outer_part(lo, hi):
        for n in range(lo, hi):
            cols = slice(n * GN, (n + 1) * GN)
            g_out[:, cols] = mm_nt(wp[...], g_ref[cols, :]).astype(BF)

    n_go = I * J // GN
    g_outer_part(0, n_go // 2)

    far_row, far_col = row_of(0, True, False), col_of(0, True)
    wait_right(far_row)
    for d in range(1, n_x):
        send_right(far_row, n_x + d, row_of(d, False, False))
    send_right(far_row, n_x, sib)
    wait_left(far_col)
    for d in range(1, n_y):
        send_left(far_col, n_y + d, col_of(d, False))

    g_outer_part(n_go // 2, n_go)

    HB = n_col // 2 * B
    HI = I // 2

    def turn_left(z, h):
        for k in range(HB // S):
            left_t[h, :, k * S:(k + 1) * S] = left[aligned(z * HB + k * S, S, S), :].T

    def right_grad(z, h, p):
        rhs = jnp.concatenate([
            jnp.concatenate([
                g_out[(2 * p + a) * C:(2 * p + a + 1) * C, aligned((z * HI + i) * J, J, J)]
                for a in range(2)], axis=1)
            for i in range(HI)], axis=0)
        return mm(left_t[h], rhs)

    for d in range(1, n_y):
        wait_left(col_of(d, False))
    turn_left(zl, 0)
    for p in range(C // 2):
        dr_acc[:, 2 * p * J:(2 * p + 2) * J] = right_grad(zl, 0, p)

    for d in range(1, n_x):
        block = row_of(d, False, False)
        wait_right(block)
        send_right(block, 2 * n_x + d, sib)
    for d in range(1, n_y):
        wait_left(col_of(d, True))
    turn_left(1 - zl, 1)
    for p in range(C // 2):
        if p == 0:
            for d in range(1, n_x):
                block = row_of(d, True, False)
                wait_right(block)
                send_right(block, 3 * n_x + d, sib)
        acc = (dr_acc[:, 2 * p * J:(2 * p + 2) * J] + right_grad(1 - zl, 1, p)) * inv
        tiles = [acc[:, a * J:(a + 1) * J].T for a in range(2)]
        for q in range(n_row):
            blk = jnp.concatenate([t[q * T:(q + 1) * T] for t in tiles], axis=0)
            dr_out[q % 2, q // 2, p * 2 * T:(p + 1) * 2 * T, :] = blk.astype(BF)
    to_sib = remote(dr_out.at[1 - core], dr_sib, dr_s.at[0], dr_r.at[n_chip], row=sib)
    send(to_sib)

    for far in (False, True):
        for d in range(n_x):
            wait_right(row_of(d, far, True))
    def right_step(h, _):
        parts = [right_in[q, aligned(h * 2 * T, 2 * T, 2 * T), :].astype(F32) for q in range(n_row)]
        for a in range(2):
            tile = jnp.concatenate([p[a * T:(a + 1) * T] for p in parts], axis=0)
            right[aligned((2 * h + a) * J, J, J), :] = tile.astype(BF)
        return 0
    lax.fori_loop(0, C // 2, right_step, 0)

    def right_grad_out():
        to_sib.wait_recv()
        def pair_step(q, _):
            dr_sib[q] = (dr_out[core, q].astype(F32) + dr_sib[q].astype(F32)).astype(BF)
            return 0
        lax.fori_loop(0, n_chip, pair_step, 0)
        for d in range(1, n_chip):
            peer = other_chip(d)
            send(remote(dr_sib.at[peer], dr_in.at[chip], dr_s.at[d], dr_r.at[chip], row=peer * 2 + core))

    for k in range(n_col):
        owner = other_col(k + 1) if k < n_col - 1 else col
        lhs = jnp.concatenate([
            jnp.concatenate([
                g_out[e * C:(e + 1) * C, aligned((owner * T + t) * J, J, J)] for t in range(T)], axis=0)
            for e in range(C)], axis=1)
        dl_out[owner] = (mm(lhs, right[...]) * inv).astype(BF)
        if k == n_col // 2 - 1:
            right_grad_out()
        if k < n_col - 1:
            send(remote(dl_out.at[owner], dl_in.at[col], dl_s.at[k], dl_r.at[col], col=owner))

    RB = I * C // 2
    NB = 4 * J
    for k in range(2):
        for n in range(C * J // NB):
            res = mm_nt(left[k * RB:(k + 1) * RB, :], right[n * NB:(n + 1) * NB, :])
            buf[k * RB:(k + 1) * RB, n * NB:(n + 1) * NB] = res.astype(BF)

    HW = CC // 2
    QE = C // 4

    def dw_quarter(e0):
        lhs = jnp.concatenate([
            jnp.concatenate([
                buf[i * C:(i + 1) * C, aligned((e0 + e) * J, J, J)] for e in range(QE)], axis=0)
            for i in range(I)], axis=1)
        return mm(lhs, g_ref[...])

    for q in range(2):
        rows = slice(q * HW // 2, (q + 1) * HW // 2)
        dw_give[rows, :] = dw_quarter((1 - core) * 2 * QE + q * QE).astype(BF)
    dw_to_sib = remote(dw_give, dw_sib, d1_s, d1_r, row=sib)
    send(dw_to_sib)
    for q in range(2):
        rows = slice(q * HW // 2, (q + 1) * HW // 2)
        dw_own[rows, :] = dw_quarter(core * 2 * QE + q * QE)

    RW = HW // n_col
    dw_to_sib.wait_recv()
    dw_pair[...] = (dw_own[...] + dw_sib[...].astype(F32)).astype(BF).reshape(n_col, RW, K)
    for d in range(1, n_col):
        peer = other_col(d)
        send(remote(dw_pair.at[peer], dw_in.at[col], d2_s.at[d], d2_r.at[col], col=peer))

    dl_sum = dl_out[col].astype(F32)
    for d in range(1, n_col):
        src = lax.rem(col + n_col - d, n_col)
        remote(dl_in.at[src], dl_in.at[src], dl_s.at[0], dl_r.at[src], col=src).wait_recv()
        dl_sum = dl_sum + dl_in[src].astype(F32)
    dl_own[...] = dl_sum.astype(BF)
    dr_sum = dr_sib[chip].astype(F32)
    for d in range(1, n_chip):
        src = lax.rem(chip + n_chip - d, n_chip)
        remote(dr_in.at[src], dr_in.at[src], dr_s.at[d], dr_r.at[src], row=src * 2 + core).wait_recv()
        dr_sum = dr_sum + dr_in[src].astype(F32)
    dr_own[...] = dr_sum

    gain = jnp.zeros((1, M), F32)
    wgrad = jnp.zeros((2 * C, M), F32)
    for t in range(T):
        dcat = jnp.concatenate(
            [dl_own[t * C:(t + 1) * C, :], dr_own[pl.ds(t, C, stride=T), :].astype(BF)], axis=0)
        wgrad = wgrad + mm(dcat, nm[t])
        dn = mm_tn(dcat, wcat)
        xhat = xh[t]
        gain = gain + jnp.sum(dn * xhat, axis=0, keepdims=True)
        hid = dn * gamma
        m1 = jnp.mean(hid, axis=1, keepdims=True)
        m2 = jnp.mean(hid * xhat, axis=1, keepdims=True)
        rstd = rs[t]
        rstd = jnp.concatenate([rstd] * wide, axis=1)
        grad = rstd * (hid - m1 - xhat * m2)
        for a in range(wide):
            xs[a, pl.ds(t, S, stride=T), :] = grad[:, a * K:(a + 1) * K]
    grads = jnp.concatenate([xs[a] for a in range(wide)], axis=1)
    ag_buf[...] = grads.reshape(S, T, M).astype(BF)
    ag_copy = pltpu.make_async_copy(ag_buf, ag_hbm, ag_sem)
    ag_copy.start()

    RS = 2 * C
    for a in range(wide):
        sm_own[a, 0:RS, :] = wgrad[:, a * K:(a + 1) * K]
        sm_own[a, RS:RS + 16, :] = jnp.broadcast_to(gain[:, a * K:(a + 1) * K], (16, K))
    sm_to_sib = remote(sm_own.at[1 - core], sm_sib, s1_s, s1_r, row=sib)
    send(sm_to_sib)

    def sum_chips(own, got, ss, rr):
        total = own
        for d in range(1, n_chip):
            src = lax.rem(chip + n_chip - d, n_chip)
            remote(got.at[src], got.at[src], ss.at[d], rr.at[src], row=src * 2 + core).wait_recv()
            total = total + got[src].astype(F32)
        return total

    def sum_cols(own, got, ss, rr):
        total = own
        for d in range(1, n_col):
            src = lax.rem(col + n_col - d, n_col)
            remote(got.at[src], got.at[src], ss.at[d], rr.at[src], col=src).wait_recv()
            total = total + got[src].astype(F32)
        return total

    def to_chips(src, dst, ss, rr):
        for d in range(1, n_chip):
            peer = other_chip(d) * 2 + core
            send(remote(src, dst.at[chip], ss.at[d], rr.at[chip], row=peer))

    def to_cols(src, dst, ss, rr):
        for d in range(1, n_col):
            send(remote(src, dst.at[col], ss.at[d], rr.at[col], col=other_col(d)))

    def z_step(p):
        rhs = jnp.concatenate([
            jnp.concatenate([
                buf[(2 * p + a) * C:(2 * p + a + 1) * C, e * J:(e + 1) * J] for e in range(C)], axis=0)
            for a in range(2)], axis=1)
        res = mm(wpt[...], rhs) * inv
        for a in range(2):
            z_buf[(2 * p + a) * J:(2 * p + a + 1) * J, :] = res[:, a * J:(a + 1) * J].T.astype(BF)

    z_copies = []
    def z_part(n, of):
        lo, hi = n * (I // 2) // of, (n + 1) * (I // 2) // of
        for p in range(lo, hi):
            z_step(p)
        rows = pl.ds(lo * 2 * J, (hi - lo) * 2 * J)
        c = pltpu.make_async_copy(z_buf.at[rows], z_hbm.at[rows], z_sem.at[n])
        c.start()
        z_copies.append(c)

    z_part(0, 4)
    sm_to_sib.wait_recv()
    sm_give[...] = sm_own[core] + sm_sib[...]
    sm_out[0] = sm_give[...].astype(BF)
    to_cols(sm_out.at[0], sm_col, s2_s, s2_r)
    z_part(1, 4)
    own = dw_pair[col].astype(F32)
    dw_blk[0] = sum_cols(own, dw_in, d2_s, d2_r).astype(BF)
    to_chips(dw_blk.at[0], dw_chip, d3_s, d3_r)
    z_part(2, 4)
    sm_sum[...] = sum_cols(sm_give[...], sm_col, s2_s, s2_r)
    sm_out[1] = sm_sum[...].astype(BF)
    to_chips(sm_out.at[1], sm_chip, s3_s, s3_r)
    z_part(3, 4)
    dw_blk[1] = (sum_chips(dw_blk[0].astype(F32), dw_chip, d3_s, d3_r) * inv).astype(BF)
    def give_dw(slot, **where):
        send(remote(dw_blk.at[1], dw_full.at[core, col], d4_s.at[slot], d4_r.at[core, col], **where))

    for d in range(1, n_col):
        give_dw(d, col=other_col(d))
        give_dw(n_col + d, row=sib, col=other_col(d))
    give_dw(0, row=sib)
    dw_full[core, col] = dw_blk[1]
    sm_half[core] = sum_chips(sm_sum[...], sm_chip, s3_s, s3_r)
    sm_back = remote(sm_half.at[core], sm_half.at[core], s4_s, s4_r.at[core], row=sib)
    send(sm_back)
    def wait_dw(h, src):
        got = dw_full.at[h, src]
        remote(got, got, d4_s.at[0], d4_r.at[h, src], row=sib).wait_recv()

    for d in range(1, n_col):
        wait_dw(core, lax.rem(col + n_col - d, n_col))

    def put_dw(h):
        per = RW // C
        for e in range(C // 2):
            part = dw_full[h, e // per, (e % per) * C:(e % per + 1) * C, :]
            dwo[pl.ds(h * (C // 2) + e, C, stride=C), :] = part.astype(F32)

    put_dw(core)

    got = sm_half.at[1 - core]
    remote(got, got, s4_s, s4_r.at[1 - core], row=sib).wait_recv()
    for a in range(wide):
        lanes = slice(a * K, (a + 1) * K)
        wl[:, lanes] = sm_half[a, 0:C, :]
        wr[:, lanes] = sm_half[a, C:2 * C, :]
        gain_buf[:, lanes] = sm_half[a, RS:RS + 1, :]
    outs = []

    def put(src, dst):
        outs.append(pltpu.make_async_copy(src, dst, out_sem.at[len(outs)]))
        outs[-1].start()

    put(wl, wl_hbm)
    put(wr, wr_hbm)
    put(gain_buf, gain_hbm)
    for d in range(n_col):
        wait_dw(1 - core, lax.rem(col + n_col - d, n_col))
    put_dw(1 - core)
    put(dwo, dwo_hbm)
    for c in outs:
        c.wait()

    ag_copy.wait()
    for c in z_copies:
        c.wait()
    for c in pending:
        c.wait_send()


def settle_kernel(*refs):
    n = (len(refs) - 2) // 3
    srcs, dsts, held = refs[:n], refs[n:2 * n], refs[2 * n:3 * n]
    in_sems, out_sems = refs[3 * n:]
    loads, stores = [], []
    for src, dst, mid in zip(srcs, dsts, held):
        parts = 4 if src.shape[0] >= 4096 else 1
        rows = src.shape[0] // parts
        for p in range(parts):
            part = pl.ds(p * rows, rows)
            k = len(loads)
            loads.append(pltpu.make_async_copy(src.at[part], mid.at[part], in_sems.at[k]))
            stores.append(pltpu.make_async_copy(mid.at[part], dst.at[part], out_sems.at[k]))
            loads[-1].start()
    for load, store in zip(loads, stores):
        load.wait()
        store.start()
    for store in stores:
        store.wait()


def settle(arrays):
    hb = pl.BlockSpec(memory_space=pl.ANY)
    sems = pltpu.SemaphoreType.DMA((len(arrays) + 3,))
    return pl.pallas_call(
        settle_kernel,
        out_shape=tuple(jax.ShapeDtypeStruct(a.shape, a.dtype) for a in arrays),
        in_specs=[hb] * len(arrays),
        out_specs=(hb,) * len(arrays),
        scratch_shapes=[pltpu.VMEM(a.shape, a.dtype) for a in arrays] + [sems, sems],
        compiler_params=pltpu.CompilerParams(vmem_limit_bytes=62 * 1024 * 1024),
    )(*arrays)


def on_device(n_row, n_col, x, gamma, w1, w2, wo, cot):
    S, T, M = x.shape
    C = w1.shape[1]
    CC, K = wo.shape
    I, J = cot.shape[0], cot.shape[1] * cot.shape[2]
    B = T * C
    n_chip = n_row // 2
    RW = CC // 2 // n_col
    RS = 2 * C + 16
    one = pltpu.SemaphoreType.DMA
    V = lambda shape, dtype: pltpu.VMEM(shape, dtype)
    D = lambda n: pltpu.SemaphoreType.DMA((n,))
    hb = pl.BlockSpec(memory_space=pl.ANY)
    parts = pl.pallas_call(
        functools.partial(kernel, n_row, n_col),
        out_shape=(
            jax.ShapeDtypeStruct((I * J, K), BF),
            jax.ShapeDtypeStruct((S, T, M), BF),
            jax.ShapeDtypeStruct((C, M), F32),
            jax.ShapeDtypeStruct((C, M), F32),
            jax.ShapeDtypeStruct((CC, K), F32),
            jax.ShapeDtypeStruct((1, M), F32),
        ),
        in_specs=[hb] * 6,
        out_specs=(hb,) * 6,
        scratch_shapes=[
            V((S, T, M), BF),
            V((1, M), F32),
            V((C, M), BF),
            V((C, M), BF),
            V((CC, K), BF),
            V((I * J, K), BF),
            V((M // K, S * T, K), F32),
            V((T, S, M), F32),
            V((T, S, M), BF),
            V((T, S, K), F32),
            V((CC, K), BF),
            V((K, CC), BF),
            V((CC, K), F32),
            V((B, S), F32),
            V((n_row, B, S), BF),
            V((C * J, S), BF),
            V((I * C, S), BF),
            V((2, S, I * C // 2), BF),
            V((CC, I * J), BF),
            V((I * C, C * J), BF),
            V((n_col, B, S), BF),
            V((n_col, B, S), BF),
            V((S, C * J), F32),
            V((2, n_chip, B, S), BF),
            V((n_chip, B, S), BF),
            V((n_chip, B, S), BF),
            V((B, S), BF),
            V((B, S), F32),
            V((CC // 2, K), BF),
            V((CC // 2, K), BF),
            V((CC // 2, K), F32),
            V((n_col, RW, K), BF),
            V((n_col, RW, K), BF),
            V((2, RW, K), BF),
            V((n_chip, RW, K), BF),
            V((2, n_col, RW, K), BF),
            V((RS, K), F32),
            V((RS, K), F32),
            V((2, RS, K), F32),
            V((2, RS, K), BF),
            V((n_col, RS, K), BF),
            V((RS, K), F32),
            V((n_chip, RS, K), BF),
            V((2, RS, K), F32),
            V((I * J, K), BF),
            V((S, T, M), BF),
            V((C, M), F32),
            V((C, M), F32),
            V((CC, K), F32),
            V((1, M), F32),
            D(5), one, D(4), one, D(4),
            D(n_row), D(n_row), D(n_col), D(n_col), D(n_col), D(n_col), D(n_chip), D(n_chip + 1),
            one, one, D(n_col), D(n_col), D(n_chip), D(n_chip), D(2 * n_col), pltpu.SemaphoreType.DMA((2, n_col)),
            one, one, D(n_col), D(n_col), D(n_chip), D(n_chip), one, D(2),
        ],
        compiler_params=pltpu.CompilerParams(
            collective_id=0, has_side_effects=True, vmem_limit_bytes=56 * 1024 * 1024,
        ),
    )(x, gamma.reshape(1, M), w1.T, w2.T, wo, cot.reshape(I * J, K))
    z, ag, wl, wr, dwo, gain = settle(parts)
    return z.reshape(cot.shape), ag, wl.T, wr.T, dwo, gain.reshape(M)


def solution(mesh):
    placed = (P(None, ("row", "col"), None), P(), P(), P(), P(), P("row", None, "col", None))
    return jax.shard_map(
        functools.partial(on_device, mesh.shape["row"], mesh.shape["col"]),
        mesh=mesh,
        in_specs=placed,
        out_specs=(P("row", None, "col", None), P(None, ("row", "col"), None), P(), P(), P(), P()),
        check_vma=False,
    )
```
